512 devices in a mesh: cfg: 2 (over core), tower: 4 (over z_hi), seq: 64 (over z_lo, x, y).
Axes of the slice: x: 4, y: 8, z: 8 (z_hi: 4, z_lo: 2; z = z_hi * 2 + z_lo), core: 2. Of those that a mesh axis runs over, the one named last changes fastest.
Arguments:
- query_self: bfloat16 [2, 4096, 2048], P('cfg', ('tower', 'seq')), may hold values from -320 to 320
- query_cross: bfloat16 [2, 4096, 2048], P('cfg', ('tower', 'seq')), may hold values from -320 to 320
- key_vectors: bfloat16 [2, 4096, 2048], P('cfg', ('tower', 'seq')), may hold values from -13 to 13
- values: bfloat16 [2, 4096, 2048], P('cfg', ('tower', 'seq')), may hold values from -6 to 6
- positions: int32 [4096], P(('tower', 'seq')), may hold values from 0 to 155, as said below
- counts: int32 [256], replicated, may hold values from 8 to 16, as said below
- guidance: float32 [1], replicated, may hold values from 1.5 to 3.5
Outputs:
- guided: bfloat16 [4096, 2048], P(('tower', 'seq'), 'cfg')
The draws below stay inside these ranges and needn't reach their ends.
Inputs may be any that keep to these rules, and one draw needn't show every extreme that they name: `positions`: integer times on one clock for video and audio tokens, never falling along the video tokens and along the audio tokens; the video tokens of one latent frame share a time. `counts`: valid tokens of each device; a device's slots beyond its count are padding.
All inputs are finite; a program needn't handle non-finite values.
Results may differ from the reference program's by a relative error of at most 0.029.
Values may be sent and summed in bfloat16 or wider, within the bound.
A program may use at most 64 MiB of HBM per device.

```python
import math
import jax
import jax.numpy as jnp
from jax import lax

HEADS = 16
DHEAD = 128
TOK_DEV = 16
FRAMES = 32
LV = 3072
LA = 1024
TOKENS = 4096
N_TOWER = 4
N_SEQ = 64


def rotate_by(matrix, delta):
    half_dim = DHEAD // 2
    frequency = 10000.0 ** (-(jnp.arange(half_dim, dtype=jnp.float32) * 2.0 / DHEAD))
    angles = delta.astype(jnp.float32)[:, None] * frequency[None, :]
    cosine = jnp.cos(angles)[None, :, None, :]
    sine_part = jnp.sin(angles)[None, :, None, :]
    heads_f32 = matrix.reshape(2, TOKENS, HEADS, DHEAD)
    front_half = heads_f32[..., :half_dim]
    back_half = heads_f32[..., half_dim:]
    rotated = jnp.concatenate([front_half * cosine - back_half * sine_part, back_half * cosine + front_half * sine_part], axis=-1)
    return rotated.reshape(2, TOKENS, HEADS * DHEAD)


def shared_draws(key, emphasis):
    frame_steps = jax.random.randint(jax.random.fold_in(key, 1), (FRAMES,), 3, 6)
    frame_time = jnp.cumsum(frame_steps) - frame_steps[0]
    frame_index = jnp.arange(FRAMES, dtype=jnp.int32)
    frame_time = jnp.where(frame_index == FRAMES - 1, 5 * (FRAMES - 1), frame_time)
    video_index = jnp.arange(LV, dtype=jnp.int32)
    video_time = frame_time[video_index // (LV // FRAMES)]
    audio_index = jnp.arange(LA, dtype=jnp.int32)
    audio_time = audio_index * frame_time[FRAMES - 1] // LA + jax.random.randint(jax.random.fold_in(key, 2), (LA,), 0, 2)
    audio_time = jax.lax.cummax(audio_time.astype(jnp.int32), axis=0)
    positions = jnp.concatenate([video_time, audio_time]).astype(jnp.int32)
    shape = (2, TOKENS, HEADS * DHEAD)
    self_base = jnp.clip(jax.random.normal(jax.random.fold_in(key, 3), shape, jnp.float32), -6.0, 6.0) * 1.5
    cross_base = jnp.clip(jax.random.normal(jax.random.fold_in(key, 4), shape, jnp.float32), -6.0, 6.0) * 1.5
    key_base = jnp.clip(jax.random.normal(jax.random.fold_in(key, 5), shape, jnp.float32), -6.0, 6.0) * 1.5
    chosen = jax.random.randint(jax.random.fold_in(key, 6), (TOKENS,), 0, 32) == 0
    strength = (12 + 4 * jax.random.randint(jax.random.fold_in(key, 7), (TOKENS,), 0, 4)).astype(jnp.float32)
    token_index = jnp.arange(TOKENS, dtype=jnp.int32)
    active = emphasis > 0.0
    before_index = jnp.maximum(token_index - 1, 0)
    lifted = rotate_by(key_base[:, before_index], positions[before_index] - positions) * (1.0 + 0.08 / strength[before_index])[None, :, None]
    second_use = (token_index % 2 == 1) & chosen[before_index] & active
    key_final = jnp.where(second_use[None, :, None], lifted, key_base)
    self_use = (token_index % 4 == 0) & chosen & active
    query_self = jnp.where(self_use[None, :, None], emphasis * strength[None, :, None] * key_base, self_base)
    partner = jnp.where(token_index < LV, LV + token_index % LA, token_index - LV)
    cross_use = (token_index % 4 == 2) & chosen[partner] & active
    aimed = rotate_by(key_base[:, partner], positions[partner] - positions) * (emphasis * strength[partner])[None, :, None]
    query_cross = jnp.where(cross_use[None, :, None], aimed, cross_base)
    return (positions, query_self, query_cross, key_final)


def draw_query_self(key, part):
    emphasis = 0.0
    return shared_draws(key, emphasis)[1].astype(jnp.bfloat16)


def draw_query_cross(key, part):
    emphasis = 0.0
    return shared_draws(key, emphasis)[2].astype(jnp.bfloat16)


def draw_key_vectors(key, part):
    emphasis = 0.0
    return shared_draws(key, emphasis)[3].astype(jnp.bfloat16)


def draw_positions(key, part):
    return shared_draws(key, 0.0)[0]


def draw_counts(key, part):
    key = jax.random.fold_in(key, 41)
    device_count = N_TOWER * N_SEQ
    drawn = jax.random.randint(jax.random.fold_in(key, 1), (device_count,), TOK_DEV // 2, TOK_DEV + 1)
    full_at = jax.random.randint(jax.random.fold_in(key, 2), (), 0, device_count)
    return jnp.where(jnp.arange(device_count, dtype=jnp.int32) == full_at, TOK_DEV, drawn).astype(jnp.int32)


def level_of(own_key, extent, cuts, least, largest):
    gain, own = 1.0, jax.random.fold_in(own_key, 6)
    for dim, shards_of in cuts:
        steps = jnp.exp(jax.random.uniform(jax.random.fold_in(own, dim), (shards_of,), jnp.float32, least / len(cuts), largest / len(cuts)))
        gain = gain * jnp.repeat(steps, extent[dim] // shards_of).reshape([-1 if axis == dim else 1 for axis in range(len(extent))])
    return gain


def scatter_about(key, extent, spread, limit, cuts=(), held_as=jnp.bfloat16):
    entries = jax.random.normal(key, extent, jnp.float32) * spread
    if len(cuts) > 0:
        entries = level_of(key, extent, cuts, -0.22, 0.18) * entries
    return jnp.clip(entries, min=-limit, max=limit).astype(held_as)


def setup_inputs(seed: int = 0) -> dict:
    seeds = jax.random.split(jax.random.key(seed), 8)
    return {
        "query_self": draw_query_self(jax.random.fold_in(seeds[7], 71), 0),
        "query_cross": draw_query_cross(jax.random.fold_in(seeds[7], 71), 0),
        "key_vectors": draw_key_vectors(jax.random.fold_in(seeds[7], 71), 0),
        "values": scatter_about(seeds[3], (2, TOKENS, HEADS * DHEAD), 1.0, 6.0, ((0, 2), (1, 256))),
        "positions": draw_positions(jax.random.fold_in(seeds[7], 71), 0),
        "counts": draw_counts(jax.random.fold_in(seeds[7], 71), 0),
        "guidance": jnp.clip(jax.random.uniform(seeds[6], (1,), jnp.float32, 1.5, 3.5), 1.5, 3.5),
    }


def rotate_heads(matrix, positions):
    token_count = matrix.shape[0]
    half_dim = DHEAD // 2
    frequency = 10000.0 ** (-(jnp.arange(half_dim, dtype=jnp.float32) * 2.0 / DHEAD))
    angles = positions.astype(jnp.float32)[:, None] * frequency[None, :]
    cosine = jnp.cos(angles)[:, None, :]
    sine_part = jnp.sin(angles)[:, None, :]
    heads_f32 = matrix.astype(jnp.float32).reshape(token_count, HEADS, DHEAD)
    front_half = heads_f32[..., :half_dim]
    back_half = heads_f32[..., half_dim:]
    rotated = jnp.concatenate([front_half * cosine - back_half * sine_part, back_half * cosine + front_half * sine_part], axis=-1)
    return rotated.reshape(token_count, HEADS * DHEAD).astype(jnp.bfloat16)

def attend_all(queries, key_rows, value_rows, key_valid):
    query_count = queries.shape[0]
    block_size = math.gcd(query_count, 512)
    scale_factor = 1.0 / math.sqrt(DHEAD)

    def one_head(head_at):
        start = head_at * DHEAD
        head_query = lax.dynamic_slice_in_dim(queries, start, DHEAD, 1).reshape(query_count // block_size, block_size, DHEAD)
        head_keys = lax.dynamic_slice_in_dim(key_rows, start, DHEAD, 1)
        head_values = lax.dynamic_slice_in_dim(value_rows, start, DHEAD, 1)

        def one_block(query_rows):
            scores = jnp.dot(query_rows, head_keys.T, preferred_element_type=jnp.float32) * scale_factor
            scores = jnp.where(key_valid[None, :], scores, -jnp.inf)
            highest = lax.optimization_barrier(jnp.max(scores, axis=1, keepdims=True))
            weights = jnp.where(key_valid[None, :], jnp.exp(scores - highest), 0.0)
            weight_sum = lax.optimization_barrier(jnp.sum(weights, axis=1, keepdims=True))
            return jnp.dot(weights.astype(jnp.bfloat16), head_values, preferred_element_type=jnp.float32) / weight_sum
        return lax.map(one_block, head_query).reshape(query_count, DHEAD)
    per_head = lax.map(one_head, jnp.arange(HEADS, dtype=jnp.int32))
    return jnp.transpose(per_head, (1, 0, 2)).reshape(query_count, HEADS * DHEAD)

def reference(query_self, query_cross, key_vectors, values, positions, counts, guidance):
    token_index = jnp.arange(TOKENS, dtype=jnp.int32)
    valid = token_index % TOK_DEV < counts[token_index // TOK_DEV]
    normed_list = []
    for branch in range(2):
        rot_self = rotate_heads(query_self[branch], positions)
        rot_cross = rotate_heads(query_cross[branch], positions)
        rot_keys = rotate_heads(key_vectors[branch], positions)
        value_rows = values[branch]
        video_self = attend_all(rot_self[:LV], rot_keys[:LV], value_rows[:LV], valid[:LV])
        video_cross = attend_all(rot_cross[:LV], rot_keys[LV:], value_rows[LV:], valid[LV:])
        audio_self = attend_all(rot_self[LV:], rot_keys[LV:], value_rows[LV:], valid[LV:])
        audio_cross = attend_all(rot_cross[LV:], rot_keys[:LV], value_rows[:LV], valid[:LV])
        combined = jnp.concatenate([video_self + video_cross, audio_self + audio_cross], axis=0)
        combined = jnp.where(valid[:, None], combined, 0.0).astype(jnp.bfloat16)
        block_f32 = combined.astype(jnp.float32)
        scale_rows = lax.rsqrt(lax.optimization_barrier(jnp.mean(block_f32 * block_f32, axis=1, keepdims=True)) + 1e-06)
        normed_list.append((block_f32 * scale_rows).astype(jnp.bfloat16))
    conditional = normed_list[0].astype(jnp.float32)
    unconditional = normed_list[1].astype(jnp.float32)
    guided = unconditional + guidance[0] * (conditional - unconditional)
    return guided.astype(jnp.bfloat16)
```

```python
import math

import jax
import jax.numpy as jnp
from jax import lax
from jax.experimental import pallas as pl
from jax.experimental.pallas import tpu as pltpu
from jax.sharding import PartitionSpec as P

HEADS = 16
D = 128
TOK = 16
SCALE = 1.0 / math.sqrt(D)
MESH = pl.DeviceIdType.MESH


def loop(lo, hi, fn):
    def body(k, carry):
        fn(k)
        return carry

    lax.fori_loop(lo, hi, body, 0)


def device(x, y, z):
    return {"tower": z // 2, "seq": (z % 2) * 32 + x * 8 + y}


def kernel(
    qs_hbm, qc_hbm, k_hbm, v_hbm, pos_hbm, counts_hbm, guide_hbm,
    out_ref,
    raw, pos, counts, guide, ones,
    kv_send, kv_all, q_rot, q_z, q_all, o_send, o_recv, l_send, l_recv, normed, paired,
    load_sem, send_sem, recv_sem,
):
    cfg = lax.axis_index("cfg")
    tower = lax.axis_index("tower")
    seq = lax.axis_index("seq")
    zl, x, y = seq // 32, (seq // 8) % 4, seq % 8
    z = tower * 2 + zl

    def lo_peer(k):
        return (y + k // 2) % 8, (zl + k % 2) % 2

    def signal(target):
        pl.semaphore_signal(barrier, inc=1, device_id=target, device_id_type=MESH)

    def remote(src, dst, target, stage):
        pltpu.make_async_remote_copy(
            src_ref=src, dst_ref=dst,
            send_sem=send_sem.at[stage], recv_sem=recv_sem.at[stage],
            device_id=target, device_id_type=MESH,
        ).start()

    def local(src, dst, stage):
        pltpu.make_async_copy(src, dst, recv_sem.at[stage]).start()

    def arrived(like, stage):
        pltpu.make_async_copy(like, like, recv_sem.at[stage]).wait()

    def sent(like, stage):
        pltpu.make_async_copy(like, like, send_sem.at[stage]).wait()

    barrier = pltpu.get_barrier_semaphore()

    def greet_lo(k):
        y2, zl2 = lo_peer(k)
        signal(device(x, y2, tower * 2 + zl2))

    loop(1, 16, greet_lo)
    loop(1, 8, lambda k: signal(device(x, y, (z + k) % 8)))
    loop(1, 4, lambda k: signal(device((x + k) % 4, y, z)))
    signal({"cfg": 1 - cfg})

    loads = [
        pltpu.make_async_copy(pos_hbm, pos, load_sem.at[4]),
        pltpu.make_async_copy(counts_hbm, counts, load_sem.at[5]),
        pltpu.make_async_copy(k_hbm, raw.at[2], load_sem.at[2]),
        pltpu.make_async_copy(v_hbm, raw.at[3], load_sem.at[3]),
        pltpu.make_async_copy(qs_hbm, raw.at[0], load_sem.at[0]),
        pltpu.make_async_copy(qc_hbm, raw.at[1], load_sem.at[1]),
        pltpu.make_async_copy(guide_hbm, guide, load_sem.at[6]),
    ]
    for copy in loads:
        copy.start()
    for copy in loads:
        copy.wait()

    row = lax.broadcasted_iota(jnp.int32, (TOK, D), 0)
    lane = lax.broadcasted_iota(jnp.int32, (TOK, D), 1)
    time = jnp.zeros((TOK, D), jnp.int32)
    for i in range(TOK):
        time = jnp.where(row == i, pos[i], time)
    half = (lane % 64).astype(jnp.float32)
    frequency = jnp.exp(half * (-2.0 / D * math.log(10000.0)))
    angle = time.astype(jnp.float32) * frequency
    cosine = jnp.cos(angle)
    sine = jnp.where(lane < 64, -jnp.sin(angle), jnp.sin(angle))

    def rope(which, h):
        block = raw[which, :, h * D:(h + 1) * D].astype(jnp.float32)
        return block * cosine + pltpu.roll(block, 64, axis=1) * sine

    own_valid = row < counts[tower * 64 + seq]
    for h in range(HEADS):
        keys = rope(2, h)
        kv_send[h, 0] = jnp.where(own_valid, keys, keys[0:1, :]).astype(jnp.bfloat16)
        vals = raw[3, :, h * D:(h + 1) * D]
        kv_send[h, 1] = jnp.where(own_valid, vals.astype(jnp.float32), 0.0).astype(jnp.bfloat16)
    for h in range(HEADS):
        q_rot[0, h % 2, h // 2] = rope(0, h).astype(jnp.bfloat16)
        q_rot[1, h % 2, h // 2] = rope(1, h).astype(jnp.bfloat16)

    pl.semaphore_wait(barrier, 15 + 7 + 3 + 1)

    own_slot = y * 2 + zl

    def send_kv(k):
        y2, zl2 = lo_peer(k)
        remote(kv_send.at[y2 * 2 + zl2], kv_all.at[x, own_slot], device(x, y2, tower * 2 + zl2), 0)

    def q_for(z2):
        return q_rot.at[(z // 6 + z2 // 6) % 2, z2 % 2]

    def send_q(k):
        z2 = (z + k) % 8
        remote(q_for(z2), q_z.at[z], device(x, y, z2), 1)

    local(kv_send.at[own_slot], kv_all.at[x, own_slot], 0)
    local(q_for(z), q_z.at[z], 1)
    loop(1, 16, send_kv)
    loop(1, 8, send_q)

    def flags(i):
        count = counts[tower * 64 + (i % 2) * 32 + (i // 16) * 8 + (i // 2) % 8]
        ones[i] = jnp.where(row < count, 1.0, 0.0).astype(jnp.bfloat16)

    loop(0, 64, flags)

    arrived(kv_all.at[x], 0)
    for k in (2, 1, 3):
        remote(kv_all.at[x], kv_all.at[x], device((x + k) % 4, y, z), 2)
    arrived(q_z, 1)

    def pass_q(k):
        y2 = (y + k) % 8
        remote(q_z.at[:, y2], q_all.at[y], device(x, y2, z), 3)

    local(q_z.at[:, y], q_all.at[y], 3)
    loop(1, 8, pass_q)
    arrived(kv_all.at[pl.ds(0, 3)], 2)
    arrived(q_all, 3)

    slot = tower * HEADS + own_slot

    def attend(step):
        y2 = (y + 4 + ((step + 1) // 2) * (2 * (step % 2) - 1)) % 8
        queries = q_all[y2].reshape(8 * TOK, D)
        keys = kv_all[:, :, 0].reshape(64 * TOK, D)
        values = jnp.concatenate(
            [kv_all[:, :, 1].reshape(64 * TOK, D), ones[...].reshape(64 * TOK, D)], axis=1
        )
        scores = lax.dot_general(
            queries, keys, (((1,), (1,)), ((), ())), preferred_element_type=jnp.float32
        )
        highest = jnp.max(scores, axis=1, keepdims=True)
        weights = jnp.exp2((scores - highest) * (SCALE / math.log(2.0))).astype(jnp.bfloat16)
        total = jnp.dot(weights, values, preferred_element_type=jnp.float32)
        weight_sum = total[:, D:]
        o_send[y2] = (total[:, :D] / weight_sum).astype(jnp.bfloat16).reshape(8, TOK, D)
        level = highest * SCALE + jnp.log(weight_sum)
        l_send[y2] = jnp.transpose(level)[0:1, :]

        def send_out(k):
            z2 = (z + 4 + k) % 8
            remote(l_send.at[y2], l_recv.at[slot], device(x, y2, z2), 5)
            remote(o_send.at[y2, z2], o_recv.at[slot], device(x, y2, z2), 4)

        loop(0, 4, send_out)
        loop(5, 8, send_out)
        return y2

    def attend_other(step):
        y2 = attend(step)
        remote(l_send.at[y2], l_recv.at[slot], device(x, y2, z), 5)
        remote(o_send.at[y2, z], o_recv.at[slot], device(x, y2, z), 4)

    loop(0, 7, attend_other)
    attend(7)
    local(l_send.at[y], l_recv.at[slot], 5)
    local(o_send.at[y, z], o_recv.at[slot], 4)

    arrived(l_recv, 5)
    levels = l_recv[...].reshape(64, D)
    levels = jnp.transpose(jnp.concatenate([levels, levels], axis=0))
    mine = jnp.zeros((TOK, D), jnp.float32)
    for z2 in range(8):
        mine = jnp.where(z == z2, levels[z2 * TOK:(z2 + 1) * TOK], mine)
    per_tower = [mine[:, t * HEADS:(t + 1) * HEADS] for t in range(3)]
    top = jnp.maximum(jnp.maximum(per_tower[0], per_tower[1]), per_tower[2])
    shares = [jnp.exp(level - top) for level in per_tower]
    share_sum = shares[0] + shares[1] + shares[2]
    shares = [share / share_sum for share in shares]
    arrived(o_recv, 4)
    blocks = []
    squares = jnp.zeros((TOK, D), jnp.float32)
    for h in range(HEADS):
        block = o_recv[3 * HEADS + h].astype(jnp.float32)
        for t in range(3):
            block += shares[t][:, h:h + 1] * o_recv[t * HEADS + h].astype(jnp.float32)
        block = jnp.where(own_valid, block, 0.0).astype(jnp.bfloat16).astype(jnp.float32)
        blocks.append(block)
        squares += block * block
    mean = jnp.sum(squares, axis=1, keepdims=True) * (1.0 / (HEADS * D))
    norm = lax.rsqrt(mean + 1e-06)
    for h in range(HEADS):
        normed[h] = (blocks[h] * norm).astype(jnp.bfloat16)

    half_heads = HEADS // 2
    remote(normed.at[pl.ds((1 - cfg) * half_heads, half_heads)], paired, {"cfg": 1 - cfg}, 6)
    arrived(paired, 6)
    for h in range(half_heads):
        here = normed[cfg * half_heads + h].astype(jnp.float32)
        there = paired[h].astype(jnp.float32)
        conditional = jnp.where(cfg == 0, here, there)
        unconditional = jnp.where(cfg == 0, there, here)
        guided = unconditional + guide[0] * (conditional - unconditional)
        out_ref[:, h * D:(h + 1) * D] = guided.astype(jnp.bfloat16)

    sent(kv_send.at[pl.ds(0, 15)], 0)
    sent(q_z.at[pl.ds(0, 7)], 1)
    sent(kv_all.at[pl.ds(0, 3)], 2)
    sent(q_all.at[pl.ds(0, 7)], 3)
    sent(o_recv.at[pl.ds(0, 63)], 4)
    sent(l_recv.at[pl.ds(0, 63)], 5)
    sent(paired, 6)


def per_device(query_self, query_cross, key_vectors, values, positions, counts, guidance):
    anywhere = pl.BlockSpec(memory_space=pl.ANY)
    bf16 = jnp.bfloat16
    return pl.pallas_call(
        kernel,
        out_shape=jax.ShapeDtypeStruct((TOK, HEADS * D // 2), bf16),
        in_specs=[anywhere] * 7,
        out_specs=pl.BlockSpec(memory_space=pltpu.VMEM),
        scratch_shapes=[
            pltpu.VMEM((4, TOK, HEADS * D), bf16),
            pltpu.SMEM((TOK,), jnp.int32),
            pltpu.SMEM((256,), jnp.int32),
            pltpu.SMEM((1,), jnp.float32),
            pltpu.VMEM((64, TOK, D), bf16),
            pltpu.VMEM((HEADS, 2, TOK, D), bf16),
            pltpu.VMEM((4, HEADS, 2, TOK, D), bf16),
            pltpu.VMEM((2, 2, 8, TOK, D), bf16),
            pltpu.VMEM((8, 8, TOK, D), bf16),
            pltpu.VMEM((8, 8, TOK, D), bf16),
            pltpu.VMEM((8, 8, TOK, D), bf16),
            pltpu.VMEM((64, TOK, D), bf16),
            pltpu.VMEM((8, 1, D), jnp.float32),
            pltpu.VMEM((64, 1, D), jnp.float32),
            pltpu.VMEM((HEADS, TOK, D), bf16),
            pltpu.VMEM((HEADS // 2, TOK, D), bf16),
            pltpu.SemaphoreType.DMA((7,)),
            pltpu.SemaphoreType.DMA((7,)),
            pltpu.SemaphoreType.DMA((7,)),
        ],
        compiler_params=pltpu.CompilerParams(
            collective_id=0, has_side_effects=True, vmem_limit_bytes=32 * 1024 * 1024
        ),
        name="twin_attention",
    )(query_self[0], query_cross[0], key_vectors[0], values[0], positions, counts, guidance)


def solution(mesh):
    return jax.shard_map(
        per_device,
        mesh=mesh,
        in_specs=(
            P("cfg", ("tower", "seq"), None),
            P("cfg", ("tower", "seq"), None),
            P("cfg", ("tower", "seq"), None),
            P("cfg", ("tower", "seq"), None),
            P(("tower", "seq")),
            P(),
            P(),
        ),
        out_specs=P(("tower", "seq"), "cfg"),
        check_vma=False,
    )
```

```python
import math

import jax
import jax.numpy as jnp
from jax import lax
from jax.experimental import pallas as pl
from jax.experimental.pallas import tpu as pltpu
from jax.sharding import PartitionSpec as P

HEADS = 16
D = 128
TOK = 16
SCALE = 1.0 / math.sqrt(D)
MESH = pl.DeviceIdType.MESH


def loop(lo, hi, fn):
    def body(k, carry):
        fn(k)
        return carry

    lax.fori_loop(lo, hi, body, 0)


def device(x, y, z):
    return {"tower": z // 2, "seq": (z % 2) * 32 + x * 8 + y}


def kernel(
    qs_hbm, qc_hbm, k_hbm, v_hbm, pos_hbm, counts_hbm, guide_hbm,
    out_ref,
    raw, pos, counts, guide, ones,
    kv_send, kv_all, q_rot, q_z, q_all, keys_t, o_send, o_recv, l_send, l_recv, normed, paired,
    load_sem, send_sem, recv_sem,
):
    cfg = lax.axis_index("cfg")
    tower = lax.axis_index("tower")
    seq = lax.axis_index("seq")
    zl, x, y = seq // 32, (seq // 8) % 4, seq % 8
    z = tower * 2 + zl

    def lo_peer(k):
        return (y + k // 2) % 8, (zl + k % 2) % 2

    def signal(target):
        pl.semaphore_signal(barrier, inc=1, device_id=target, device_id_type=MESH)

    def remote(src, dst, target, stage):
        pltpu.make_async_remote_copy(
            src_ref=src, dst_ref=dst,
            send_sem=send_sem.at[stage], recv_sem=recv_sem.at[stage],
            device_id=target, device_id_type=MESH,
        ).start()

    def local(src, dst, stage):
        pltpu.make_async_copy(src, dst, recv_sem.at[stage]).start()

    def arrived(like, stage):
        pltpu.make_async_copy(like, like, recv_sem.at[stage]).wait()

    def sent(like, stage):
        pltpu.make_async_copy(like, like, send_sem.at[stage]).wait()

    barrier = pltpu.get_barrier_semaphore()

    def greet_lo(k):
        y2, zl2 = lo_peer(k)
        signal(device(x, y2, tower * 2 + zl2))

    loop(1, 16, greet_lo)
    loop(1, 8, lambda k: signal(device(x, y, (z + k) % 8)))
    loop(1, 4, lambda k: signal(device((x + k) % 4, y, z)))
    signal({"cfg": 1 - cfg})

    loads = [
        pltpu.make_async_copy(pos_hbm, pos, load_sem.at[4]),
        pltpu.make_async_copy(counts_hbm, counts, load_sem.at[5]),
        pltpu.make_async_copy(k_hbm, raw.at[2], load_sem.at[2]),
        pltpu.make_async_copy(v_hbm, raw.at[3], load_sem.at[3]),
        pltpu.make_async_copy(qs_hbm, raw.at[0], load_sem.at[0]),
        pltpu.make_async_copy(qc_hbm, raw.at[1], load_sem.at[1]),
        pltpu.make_async_copy(guide_hbm, guide, load_sem.at[6]),
    ]
    for copy in loads:
        copy.start()
    for copy in loads:
        copy.wait()

    row = lax.broadcasted_iota(jnp.int32, (TOK, D), 0)
    lane = lax.broadcasted_iota(jnp.int32, (TOK, D), 1)
    time = jnp.zeros((TOK, D), jnp.int32)
    for i in range(TOK):
        time = jnp.where(row == i, pos[i], time)
    half = (lane % 64).astype(jnp.float32)
    frequency = jnp.exp(half * (-2.0 / D * math.log(10000.0)))
    angle = time.astype(jnp.float32) * frequency
    cosine = jnp.cos(angle)
    sine = jnp.where(lane < 64, -jnp.sin(angle), jnp.sin(angle))

    def rope(which, h):
        block = raw[which, :, h * D:(h + 1) * D].astype(jnp.float32)
        return block * cosine + pltpu.roll(block, 64, axis=1) * sine

    own_valid = row < counts[tower * 64 + seq]
    for h in range(HEADS):
        keys = rope(2, h)
        kv_send[h, 0] = jnp.where(own_valid, keys, keys[0:1, :]).astype(jnp.bfloat16)
        vals = raw[3, :, h * D:(h + 1) * D]
        kv_send[h, 1] = jnp.where(own_valid, vals.astype(jnp.float32), 0.0).astype(jnp.bfloat16)
    for h in range(HEADS):
        q_rot[0, h % 2, h // 2] = rope(0, h).astype(jnp.bfloat16)
        q_rot[1, h % 2, h // 2] = rope(1, h).astype(jnp.bfloat16)

    pl.semaphore_wait(barrier, 15 + 7 + 3 + 1)

    own_slot = y * 2 + zl

    def send_kv(k):
        y2, zl2 = lo_peer(k)
        remote(kv_send.at[y2 * 2 + zl2], kv_all.at[x, own_slot], device(x, y2, tower * 2 + zl2), 0)

    def q_for(z2):
        return q_rot.at[(z // 6 + z2 // 6) % 2, z2 % 2]

    def send_q(k):
        z2 = (z + k) % 8
        remote(q_for(z2), q_z.at[z], device(x, y, z2), 1)

    local(kv_send.at[own_slot], kv_all.at[x, own_slot], 0)
    local(q_for(z), q_z.at[z], 1)
    loop(1, 16, send_kv)
    loop(1, 8, send_q)

    def flags(i):
        count = counts[tower * 64 + (i % 2) * 32 + (i // 16) * 8 + (i // 2) % 8]
        ones[i] = jnp.where(row < count, 1.0, 0.0).astype(jnp.bfloat16)

    loop(0, 64, flags)

    arrived(kv_all.at[x], 0)
    for k in (2, 1, 3):
        remote(kv_all.at[x], kv_all.at[x], device((x + k) % 4, y, z), 2)
    arrived(q_z, 1)

    def pass_q(k):
        y2 = (y + k) % 8
        remote(q_z.at[:, y2], q_all.at[y], device(x, y2, z), 3)

    local(q_z.at[:, y], q_all.at[y], 3)
    loop(1, 8, pass_q)
    arrived(kv_all.at[pl.ds(0, 3)], 2)
    arrived(q_all, 3)

    slot = tower * HEADS + own_slot

    keys_t[...] = jnp.transpose(kv_all[:, :, 0].reshape(64 * TOK, D))

    def attend(y2):
        queries = q_all[y2].reshape(8 * TOK, D)
        values = jnp.concatenate(
            [kv_all[:, :, 1].reshape(64 * TOK, D), ones[...].reshape(64 * TOK, D)], axis=1
        )
        scores = jnp.dot(queries, keys_t[...], preferred_element_type=jnp.float32)
        highest = jnp.max(scores, axis=1, keepdims=True)
        weights = jnp.exp2((scores - highest) * (SCALE / math.log(2.0))).astype(jnp.bfloat16)
        total = jnp.dot(weights, values, preferred_element_type=jnp.float32)
        weight_sum = total[:, D:]
        o_send[y2] = (total[:, :D] / weight_sum).astype(jnp.bfloat16).reshape(8, TOK, D)
        level = highest * SCALE + jnp.log(weight_sum)
        l_send[y2] = jnp.transpose(level)[0:1, :]

    def send_out(y2, z2):
        remote(l_send.at[y2], l_recv.at[slot], device(x, y2, z2), 5)
        remote(o_send.at[y2, z2], o_recv.at[slot], device(x, y2, z2), 4)

    def attend_group(offsets):
        for k in offsets:
            attend((y + k) % 8)
        for k in offsets:
            y2 = (y + k) % 8
            loop(1, 8, lambda j: send_out(y2, (z + (j + 3) % 7 + 1) % 8))
            if k:
                send_out(y2, z)

    attend_group((4, 5, 3, 6))
    attend_group((2, 7, 1, 0))
    local(l_send.at[y], l_recv.at[slot], 5)
    local(o_send.at[y, z], o_recv.at[slot], 4)

    arrived(l_recv, 5)
    levels = l_recv[...].reshape(64, D)
    levels = jnp.transpose(jnp.concatenate([levels, levels], axis=0))
    mine = jnp.zeros((TOK, D), jnp.float32)
    for z2 in range(8):
        mine = jnp.where(z == z2, levels[z2 * TOK:(z2 + 1) * TOK], mine)
    per_tower = [mine[:, t * HEADS:(t + 1) * HEADS] for t in range(3)]
    top = jnp.maximum(jnp.maximum(per_tower[0], per_tower[1]), per_tower[2])
    shares = [jnp.exp(level - top) for level in per_tower]
    share_sum = shares[0] + shares[1] + shares[2]
    shares = [share / share_sum for share in shares]
    arrived(o_recv, 4)
    blocks = []
    squares = jnp.zeros((TOK, D), jnp.float32)
    for h in range(HEADS):
        block = o_recv[3 * HEADS + h].astype(jnp.float32)
        for t in range(3):
            block += shares[t][:, h:h + 1] * o_recv[t * HEADS + h].astype(jnp.float32)
        block = jnp.where(own_valid, block, 0.0).astype(jnp.bfloat16).astype(jnp.float32)
        blocks.append(block)
        squares += block * block
    mean = jnp.sum(squares, axis=1, keepdims=True) * (1.0 / (HEADS * D))
    norm = lax.rsqrt(mean + 1e-06)
    for h in range(HEADS):
        normed[h] = (blocks[h] * norm).astype(jnp.bfloat16)

    half_heads = HEADS // 2
    remote(normed.at[pl.ds((1 - cfg) * half_heads, half_heads)], paired, {"cfg": 1 - cfg}, 6)
    arrived(paired, 6)
    for h in range(half_heads):
        here = normed[cfg * half_heads + h].astype(jnp.float32)
        there = paired[h].astype(jnp.float32)
        conditional = jnp.where(cfg == 0, here, there)
        unconditional = jnp.where(cfg == 0, there, here)
        guided = unconditional + guide[0] * (conditional - unconditional)
        out_ref[:, h * D:(h + 1) * D] = guided.astype(jnp.bfloat16)

    sent(kv_send.at[pl.ds(0, 15)], 0)
    sent(q_z.at[pl.ds(0, 7)], 1)
    sent(kv_all.at[pl.ds(0, 3)], 2)
    sent(q_all.at[pl.ds(0, 7)], 3)
    sent(o_recv.at[pl.ds(0, 63)], 4)
    sent(l_recv.at[pl.ds(0, 63)], 5)
    sent(paired, 6)


def per_device(query_self, query_cross, key_vectors, values, positions, counts, guidance):
    anywhere = pl.BlockSpec(memory_space=pltpu.HBM)
    bf16 = jnp.bfloat16
    return pl.pallas_call(
        kernel,
        out_shape=jax.ShapeDtypeStruct((TOK, HEADS * D // 2), bf16),
        in_specs=[anywhere] * 7,
        out_specs=pl.BlockSpec(memory_space=pltpu.VMEM),
        scratch_shapes=[
            pltpu.VMEM((4, TOK, HEADS * D), bf16),
            pltpu.SMEM((TOK,), jnp.int32),
            pltpu.SMEM((256,), jnp.int32),
            pltpu.SMEM((1,), jnp.float32),
            pltpu.VMEM((64, TOK, D), bf16),
            pltpu.VMEM((HEADS, 2, TOK, D), bf16),
            pltpu.VMEM((4, HEADS, 2, TOK, D), bf16),
            pltpu.VMEM((2, 2, 8, TOK, D), bf16),
            pltpu.VMEM((8, 8, TOK, D), bf16),
            pltpu.VMEM((8, 8, TOK, D), bf16),
            pltpu.VMEM((D, 64 * TOK), bf16),
            pltpu.VMEM((8, 8, TOK, D), bf16),
            pltpu.VMEM((64, TOK, D), bf16),
            pltpu.VMEM((8, 1, D), jnp.float32),
            pltpu.VMEM((64, 1, D), jnp.float32),
            pltpu.VMEM((HEADS, TOK, D), bf16),
            pltpu.VMEM((HEADS // 2, TOK, D), bf16),
            pltpu.SemaphoreType.DMA((7,)),
            pltpu.SemaphoreType.DMA((7,)),
            pltpu.SemaphoreType.DMA((7,)),
        ],
        compiler_params=pltpu.CompilerParams(
            collective_id=0, has_side_effects=True, vmem_limit_bytes=32 * 1024 * 1024
        ),
        name="twin_attention",
    )(query_self[0], query_cross[0], key_vectors[0], values[0], positions, counts, guidance)


def solution(mesh):
    return jax.shard_map(
        per_device,
        mesh=mesh,
        in_specs=(
            P("cfg", ("tower", "seq"), None),
            P("cfg", ("tower", "seq"), None),
            P("cfg", ("tower", "seq"), None),
            P("cfg", ("tower", "seq"), None),
            P(("tower", "seq")),
            P(),
            P(),
        ),
        out_specs=P(("tower", "seq"), "cfg"),
        check_vma=False,
    )
```

```python
import math

import jax
import jax.numpy as jnp
from jax import lax
from jax.experimental import pallas as pl
from jax.experimental.pallas import tpu as pltpu
from jax.sharding import PartitionSpec as P

HEADS = 16
D = 128
TOK = 16
SCALE = 1.0 / math.sqrt(D)
MESH = pl.DeviceIdType.MESH


def loop(lo, hi, fn):
    def body(k, carry):
        fn(k)
        return carry

    lax.fori_loop(lo, hi, body, 0)


def device(x, y, z):
    return {"tower": z // 2, "seq": (z % 2) * 32 + x * 8 + y}


def kernel(
    qs_hbm, qc_hbm, k_hbm, v_hbm, pos_hbm, counts_hbm, guide_hbm,
    out_ref,
    raw, pos, counts, guide, ones,
    kv_send, kv_all, q_rot, q_z, q_all, keys_t, o_send, o_recv, l_send, l_recv, normed, paired,
    load_sem, send_sem, recv_sem, kv_sem, qz_sem, qy_sem,
):
    cfg = lax.axis_index("cfg")
    tower = lax.axis_index("tower")
    seq = lax.axis_index("seq")
    zl, x, y = seq // 32, (seq // 8) % 4, seq % 8
    z = tower * 2 + zl

    def lo_peer(k):
        return (y + k // 2) % 8, (zl + k % 2) % 2

    def signal(target):
        pl.semaphore_signal(barrier, inc=1, device_id=target, device_id_type=MESH)

    def remote(src, dst, target, stage, landed):
        pltpu.make_async_remote_copy(
            src_ref=src, dst_ref=dst,
            send_sem=send_sem.at[stage], recv_sem=landed,
            device_id=target, device_id_type=MESH,
        ).start()

    def local(src, dst, landed):
        pltpu.make_async_copy(src, dst, landed).start()

    def arrived(like, landed):
        pltpu.make_async_copy(like, like, landed).wait()

    def sent(like, stage):
        pltpu.make_async_copy(like, like, send_sem.at[stage]).wait()

    barrier = pltpu.get_barrier_semaphore()

    def greet_lo(k):
        y2, zl2 = lo_peer(k)
        signal(device(x, y2, tower * 2 + zl2))

    loop(1, 16, greet_lo)
    loop(1, 8, lambda k: signal(device(x, y, (z + k) % 8)))
    loop(1, 4, lambda k: signal(device((x + k) % 4, y, z)))
    signal({"cfg": 1 - cfg})

    loads = [
        pltpu.make_async_copy(pos_hbm, pos, load_sem.at[4]),
        pltpu.make_async_copy(counts_hbm, counts, load_sem.at[5]),
        pltpu.make_async_copy(k_hbm, raw.at[2], load_sem.at[2]),
        pltpu.make_async_copy(v_hbm, raw.at[3], load_sem.at[3]),
        pltpu.make_async_copy(qs_hbm, raw.at[0], load_sem.at[0]),
        pltpu.make_async_copy(qc_hbm, raw.at[1], load_sem.at[1]),
        pltpu.make_async_copy(guide_hbm, guide, load_sem.at[6]),
    ]
    for copy in loads:
        copy.start()
    for copy in loads:
        copy.wait()

    row = lax.broadcasted_iota(jnp.int32, (TOK, D), 0)
    lane = lax.broadcasted_iota(jnp.int32, (TOK, D), 1)
    time = jnp.zeros((TOK, D), jnp.int32)
    for i in range(TOK):
        time = jnp.where(row == i, pos[i], time)
    half = (lane % 64).astype(jnp.float32)
    frequency = jnp.exp(half * (-2.0 / D * math.log(10000.0)))
    angle = time.astype(jnp.float32) * frequency
    cosine = jnp.cos(angle)
    sine = jnp.where(lane < 64, -jnp.sin(angle), jnp.sin(angle))

    def rope(which, h):
        block = raw[which, :, h * D:(h + 1) * D].astype(jnp.float32)
        return block * cosine + pltpu.roll(block, 64, axis=1) * sine

    own_valid = row < counts[tower * 64 + seq]
    for h in range(HEADS):
        keys = rope(2, h)
        kv_send[h, 0] = jnp.where(own_valid, keys, keys[0:1, :]).astype(jnp.bfloat16)
        vals = raw[3, :, h * D:(h + 1) * D]
        kv_send[h, 1] = jnp.where(own_valid, vals.astype(jnp.float32), 0.0).astype(jnp.bfloat16)
    for h in range(HEADS):
        q_rot[0, h % 2, h // 2] = rope(0, h).astype(jnp.bfloat16)
        q_rot[1, h % 2, h // 2] = rope(1, h).astype(jnp.bfloat16)

    pl.semaphore_wait(barrier, 15 + 7 + 3 + 1)

    own_slot = y * 2 + zl

    def q_for(z2):
        return q_rot.at[(z // 6 + z2 // 6) % 2, z2 % 2]

    def send_kv(y2, zl2):
        remote(
            kv_send.at[y2 * 2 + zl2], kv_all.at[x, own_slot],
            device(x, y2, tower * 2 + zl2), 0, kv_sem.at[own_slot],
        )

    def send_q(z2):
        remote(q_for(z2), q_z.at[z], device(x, y, z2), 1, qz_sem.at[z])

    def pass_kv(block, source):
        for k in (2, 1, 3):
            remote(block, kv_all.at[x, source], device((x + k) % 4, y, z), 2, recv_sem.at[2])

    def pass_q(block, source):
        def pass_one(j):
            y2 = (y + (j + 3) % 7 + 1) % 8
            remote(block.at[y2], q_all.at[y, source], device(x, y2, z), 3, qy_sem.at[y])

        loop(0, 7, pass_one)
        local(block.at[y], q_all.at[y, source], qy_sem.at[y])

    for k in (4, 3, 5, 2, 6, 1, 7):
        send_kv((y + k) % 8, zl)
        send_kv((y + k) % 8, 1 - zl)
        send_q((z + k) % 8)
    send_kv(y, 1 - zl)
    local(kv_send.at[own_slot], kv_all.at[x, own_slot], kv_sem.at[own_slot])
    pass_kv(kv_send.at[own_slot], own_slot)
    pass_q(q_for(z), z)

    def flags(i):
        count = counts[tower * 64 + (i % 2) * 32 + (i // 16) * 8 + (i // 2) % 8]
        ones[i] = jnp.where(row < count, 1.0, 0.0).astype(jnp.bfloat16)

    loop(0, 64, flags)

    def kv_from(y2, zl2):
        source = y2 * 2 + zl2
        arrived(kv_all.at[x, source], kv_sem.at[source])
        pass_kv(kv_all.at[x, source], source)

    kv_from(y, 1 - zl)
    for k in (1, 7, 2, 6, 3, 5, 4):
        z2 = (z + k) % 8
        arrived(q_z.at[z2], qz_sem.at[z2])
        pass_q(q_z.at[z2], z2)
        kv_from((y + k) % 8, zl)
        kv_from((y + k) % 8, 1 - zl)
    arrived(kv_all.at[x, own_slot], kv_sem.at[own_slot])
    arrived(kv_all.at[pl.ds(0, 3)], recv_sem.at[2])

    slot = tower * HEADS + own_slot

    keys_t[...] = jnp.transpose(kv_all[:, :, 0].reshape(64 * TOK, D))

    def attend(y2):
        queries = q_all[y2].reshape(8 * TOK, D)
        values = jnp.concatenate(
            [kv_all[:, :, 1].reshape(64 * TOK, D), ones[...].reshape(64 * TOK, D)], axis=1
        )
        scores = jnp.dot(queries, keys_t[...], preferred_element_type=jnp.float32)
        highest = jnp.max(scores, axis=1, keepdims=True)
        weights = jnp.exp2((scores - highest) * (SCALE / math.log(2.0))).astype(jnp.bfloat16)
        total = jnp.dot(weights, values, preferred_element_type=jnp.float32)
        weight_sum = total[:, D:]
        o_send[y2] = (total[:, :D] / weight_sum).astype(jnp.bfloat16).reshape(8, TOK, D)
        level = highest * SCALE + jnp.log(weight_sum)
        l_send[y2] = jnp.transpose(level)[0:1, :]

    def send_out(y2, z2):
        remote(l_send.at[y2], l_recv.at[slot], device(x, y2, z2), 5, recv_sem.at[5])
        remote(o_send.at[y2, z2], o_recv.at[slot], device(x, y2, z2), 4, recv_sem.at[4])

    def attend_group(offsets):
        for k in offsets:
            arrived(q_all.at[(y + k) % 8], qy_sem.at[(y + k) % 8])
        for k in offsets:
            attend((y + k) % 8)
        for k in offsets:
            y2 = (y + k) % 8
            loop(1, 8, lambda j: send_out(y2, (z + (j + 3) % 7 + 1) % 8))
            if k:
                send_out(y2, z)

    attend_group((0, 1, 7, 2))
    attend_group((6, 3, 5, 4))
    local(l_send.at[y], l_recv.at[slot], recv_sem.at[5])
    local(o_send.at[y, z], o_recv.at[slot], recv_sem.at[4])

    arrived(l_recv, recv_sem.at[5])
    levels = l_recv[...].reshape(64, D)
    levels = jnp.transpose(jnp.concatenate([levels, levels], axis=0))
    mine = jnp.zeros((TOK, D), jnp.float32)
    for z2 in range(8):
        mine = jnp.where(z == z2, levels[z2 * TOK:(z2 + 1) * TOK], mine)
    per_tower = [mine[:, t * HEADS:(t + 1) * HEADS] for t in range(3)]
    top = jnp.maximum(jnp.maximum(per_tower[0], per_tower[1]), per_tower[2])
    shares = [jnp.exp(level - top) for level in per_tower]
    share_sum = shares[0] + shares[1] + shares[2]
    shares = [share / share_sum for share in shares]
    arrived(o_recv, recv_sem.at[4])
    blocks = []
    squares = jnp.zeros((TOK, D), jnp.float32)
    for h in range(HEADS):
        block = o_recv[3 * HEADS + h].astype(jnp.float32)
        for t in range(3):
            block += shares[t][:, h:h + 1] * o_recv[t * HEADS + h].astype(jnp.float32)
        block = jnp.where(own_valid, block, 0.0).astype(jnp.bfloat16).astype(jnp.float32)
        blocks.append(block)
        squares += block * block
    mean = jnp.sum(squares, axis=1, keepdims=True) * (1.0 / (HEADS * D))
    norm = lax.rsqrt(mean + 1e-06)
    for h in range(HEADS):
        normed[h] = (blocks[h] * norm).astype(jnp.bfloat16)

    half_heads = HEADS // 2
    remote(normed.at[pl.ds((1 - cfg) * half_heads, half_heads)], paired, {"cfg": 1 - cfg}, 6, recv_sem.at[6])
    arrived(paired, recv_sem.at[6])
    for h in range(half_heads):
        here = normed[cfg * half_heads + h].astype(jnp.float32)
        there = paired[h].astype(jnp.float32)
        conditional = jnp.where(cfg == 0, here, there)
        unconditional = jnp.where(cfg == 0, there, here)
        guided = unconditional + guide[0] * (conditional - unconditional)
        out_ref[:, h * D:(h + 1) * D] = guided.astype(jnp.bfloat16)

    sent(kv_send.at[pl.ds(0, 15)], 0)
    sent(q_z.at[pl.ds(0, 7)], 1)
    sent(kv_all.at[pl.ds(0, 3)], 2)
    sent(q_all.at[pl.ds(0, 7)], 3)
    sent(o_recv.at[pl.ds(0, 63)], 4)
    sent(l_recv.at[pl.ds(0, 63)], 5)
    sent(paired, 6)


def per_device(query_self, query_cross, key_vectors, values, positions, counts, guidance):
    anywhere = pl.BlockSpec(memory_space=pltpu.HBM)
    bf16 = jnp.bfloat16
    return pl.pallas_call(
        kernel,
        out_shape=jax.ShapeDtypeStruct((TOK, HEADS * D // 2), bf16),
        in_specs=[anywhere] * 7,
        out_specs=pl.BlockSpec(memory_space=pltpu.VMEM),
        scratch_shapes=[
            pltpu.VMEM((4, TOK, HEADS * D), bf16),
            pltpu.SMEM((TOK,), jnp.int32),
            pltpu.SMEM((256,), jnp.int32),
            pltpu.SMEM((1,), jnp.float32),
            pltpu.VMEM((64, TOK, D), bf16),
            pltpu.VMEM((HEADS, 2, TOK, D), bf16),
            pltpu.VMEM((4, HEADS, 2, TOK, D), bf16),
            pltpu.VMEM((2, 2, 8, TOK, D), bf16),
            pltpu.VMEM((8, 8, TOK, D), bf16),
            pltpu.VMEM((8, 8, TOK, D), bf16),
            pltpu.VMEM((D, 64 * TOK), bf16),
            pltpu.VMEM((8, 8, TOK, D), bf16),
            pltpu.VMEM((64, TOK, D), bf16),
            pltpu.VMEM((8, 1, D), jnp.float32),
            pltpu.VMEM((64, 1, D), jnp.float32),
            pltpu.VMEM((HEADS, TOK, D), bf16),
            pltpu.VMEM((HEADS // 2, TOK, D), bf16),
            pltpu.SemaphoreType.DMA((7,)),
            pltpu.SemaphoreType.DMA((7,)),
            pltpu.SemaphoreType.DMA((7,)),
            pltpu.SemaphoreType.DMA((16,)),
            pltpu.SemaphoreType.DMA((8,)),
            pltpu.SemaphoreType.DMA((8,)),
        ],
        compiler_params=pltpu.CompilerParams(
            collective_id=0, has_side_effects=True, vmem_limit_bytes=56 * 1024 * 1024
        ),
        name="twin_attention",
    )(query_self[0], query_cross[0], key_vectors[0], values[0], positions, counts, guidance)


def solution(mesh):
    return jax.shard_map(
        per_device,
        mesh=mesh,
        in_specs=(
            P("cfg", ("tower", "seq"), None),
            P("cfg", ("tower", "seq"), None),
            P("cfg", ("tower", "seq"), None),
            P("cfg", ("tower", "seq"), None),
            P(("tower", "seq")),
            P(),
            P(),
        ),
        out_specs=P(("tower", "seq"), "cfg"),
        check_vma=False,
    )
```

```python
import math

import jax
import jax.numpy as jnp
from jax import lax
from jax.experimental import pallas as pl
from jax.experimental.pallas import tpu as pltpu
from jax.sharding import PartitionSpec as P

HEADS = 16
D = 128
TOK = 16
SCALE = 1.0 / math.sqrt(D)
NEAR = (0, 1, 7, 2, 6, 3, 5, 4)
MESH = pl.DeviceIdType.MESH


def loop(lo, hi, fn):
    def body(k, carry):
        fn(k)
        return carry

    lax.fori_loop(lo, hi, body, 0)


def device(x, y, z):
    return {"tower": z // 2, "seq": (z % 2) * 32 + x * 8 + y}


def kernel(
    qs_hbm, qc_hbm, k_hbm, v_hbm, pos_hbm, counts_hbm, guide_hbm,
    out_ref,
    raw, pos, counts, guide, ones,
    kv_send, kv_all, q_rot, q_y, q_all, keys_t, o_send, o_recv, l_send, l_recv, normed, paired,
    load_sem, send_sem, recv_sem, kv_sem, qy_sem, qz_sem,
):
    cfg = lax.axis_index("cfg")
    tower = lax.axis_index("tower")
    seq = lax.axis_index("seq")
    zl, x, y = seq // 32, (seq // 8) % 4, seq % 8
    z = tower * 2 + zl

    def lo_peer(k):
        return (y + k // 2) % 8, (zl + k % 2) % 2

    def signal(target):
        pl.semaphore_signal(barrier, inc=1, device_id=target, device_id_type=MESH)

    def remote(src, dst, target, stage, landed):
        pltpu.make_async_remote_copy(
            src_ref=src, dst_ref=dst,
            send_sem=send_sem.at[stage], recv_sem=landed,
            device_id=target, device_id_type=MESH,
        ).start()

    def local(src, dst, landed):
        pltpu.make_async_copy(src, dst, landed).start()

    def arrived(like, landed):
        pltpu.make_async_copy(like, like, landed).wait()

    def sent(like, stage):
        pltpu.make_async_copy(like, like, send_sem.at[stage]).wait()

    barrier = pltpu.get_barrier_semaphore()

    def greet_lo(k):
        y2, zl2 = lo_peer(k)
        signal(device(x, y2, tower * 2 + zl2))

    loop(1, 16, greet_lo)
    loop(1, 8, lambda k: signal(device(x, y, (z + k) % 8)))
    loop(1, 4, lambda k: signal(device((x + k) % 4, y, z)))
    signal({"cfg": 1 - cfg})

    loads = [
        pltpu.make_async_copy(pos_hbm, pos, load_sem.at[4]),
        pltpu.make_async_copy(counts_hbm, counts, load_sem.at[5]),
        pltpu.make_async_copy(k_hbm, raw.at[2], load_sem.at[2]),
        pltpu.make_async_copy(v_hbm, raw.at[3], load_sem.at[3]),
        pltpu.make_async_copy(qs_hbm, raw.at[0], load_sem.at[0]),
        pltpu.make_async_copy(qc_hbm, raw.at[1], load_sem.at[1]),
        pltpu.make_async_copy(guide_hbm, guide, load_sem.at[6]),
    ]
    for copy in loads:
        copy.start()
    for copy in loads:
        copy.wait()

    row = lax.broadcasted_iota(jnp.int32, (TOK, D), 0)
    lane = lax.broadcasted_iota(jnp.int32, (TOK, D), 1)
    time = jnp.zeros((TOK, D), jnp.int32)
    for i in range(TOK):
        time = jnp.where(row == i, pos[i], time)
    half = (lane % 64).astype(jnp.float32)
    frequency = jnp.exp(half * (-2.0 / D * math.log(10000.0)))
    angle = time.astype(jnp.float32) * frequency
    cosine = jnp.cos(angle)
    sine = jnp.where(lane < 64, -jnp.sin(angle), jnp.sin(angle))

    def rope(which, h):
        block = raw[which, :, h * D:(h + 1) * D].astype(jnp.float32)
        return block * cosine + pltpu.roll(block, 64, axis=1) * sine

    own_valid = row < counts[tower * 64 + seq]
    for h in range(HEADS):
        keys = rope(2, h)
        kv_send[h, 0] = jnp.where(own_valid, keys, keys[0:1, :]).astype(jnp.bfloat16)
        vals = raw[3, :, h * D:(h + 1) * D]
        kv_send[h, 1] = jnp.where(own_valid, vals.astype(jnp.float32), 0.0).astype(jnp.bfloat16)
    for h in range(HEADS):
        q_rot[h // 2, 0, h % 2] = rope(0, h).astype(jnp.bfloat16)
        q_rot[h // 2, 1, h % 2] = rope(1, h).astype(jnp.bfloat16)

    pl.semaphore_wait(barrier, 15 + 7 + 3 + 1)

    own_slot = y * 2 + zl

    def send_kv(y2, zl2):
        remote(
            kv_send.at[y2 * 2 + zl2], kv_all.at[x, own_slot],
            device(x, y2, tower * 2 + zl2), 0, kv_sem.at[own_slot],
        )

    def send_q(k):
        place = NEAR.index((8 - k) % 8)
        remote(q_rot.at[(y + k) % 8], q_y.at[place], device(x, (y + k) % 8, z), 1, qy_sem.at[place])

    def pass_kv(block, source):
        for k in (2, 1, 3):
            remote(block, kv_all.at[x, source], device((x + k) % 4, y, z), 2, recv_sem.at[2])

    def q_for(z2, places):
        return q_y.at[places, (z // 6 + z2 // 6) % 2, z2 % 2]

    def pass_q(first, count):
        places = pl.ds(first, count)

        def pass_one(j):
            z2 = (z + (j + 3) % 7 + 1) % 8
            remote(q_for(z2, places), q_all.at[z, places], device(x, y, z2), 3, qz_sem.at[z])

        loop(0, 7, pass_one)
        local(q_for(z, places), q_all.at[z, places], qz_sem.at[z])

    local(q_rot.at[y], q_y.at[0], qy_sem.at[0])
    for k in (4, 3, 5, 2, 6, 1, 7):
        send_q(k)
        send_kv((y + k) % 8, zl)
        send_kv((y + k) % 8, 1 - zl)
    send_kv(y, 1 - zl)
    local(kv_send.at[own_slot], kv_all.at[x, own_slot], kv_sem.at[own_slot])
    pass_kv(kv_send.at[own_slot], own_slot)

    def flags(i):
        count = counts[tower * 64 + (i % 2) * 32 + (i // 16) * 8 + (i // 2) % 8]
        ones[i] = jnp.where(row < count, 1.0, 0.0).astype(jnp.bfloat16)

    loop(0, 64, flags)

    def kv_from(y2, zl2):
        source = y2 * 2 + zl2
        arrived(kv_all.at[x, source], kv_sem.at[source])
        pass_kv(kv_all.at[x, source], source)

    kv_from(y, 1 - zl)
    arrived(q_y.at[0], qy_sem.at[0])
    for place in range(1, 8):
        arrived(q_y.at[place], qy_sem.at[place])
        if place == 4:
            pass_q(0, 5)
        if place == 7:
            pass_q(5, 3)
        kv_from((y + NEAR[place]) % 8, zl)
        kv_from((y + NEAR[place]) % 8, 1 - zl)
    arrived(kv_all.at[x, own_slot], kv_sem.at[own_slot])
    arrived(kv_all.at[pl.ds(0, 3)], recv_sem.at[2])

    slot = tower * HEADS + own_slot
    keys_t[...] = jnp.transpose(kv_all[:, :, 0].reshape(64 * TOK, D))

    def attend(z2):
        queries = q_all[z2].reshape(8 * TOK, D)
        values = jnp.concatenate(
            [kv_all[:, :, 1].reshape(64 * TOK, D), ones[...].reshape(64 * TOK, D)], axis=1
        )
        scores = jnp.dot(queries, keys_t[...], preferred_element_type=jnp.float32)
        highest = jnp.max(scores, axis=1, keepdims=True)
        weights = jnp.exp2((scores - highest) * (SCALE / math.log(2.0))).astype(jnp.bfloat16)
        total = jnp.dot(weights, values, preferred_element_type=jnp.float32)
        weight_sum = total[:, D:]
        o_send[z2] = (total[:, :D] / weight_sum).astype(jnp.bfloat16).reshape(8, TOK, D)
        level = highest * SCALE + jnp.log(weight_sum)
        l_send[z2] = jnp.transpose(level)[0:1, :]

    def send_out(z2, place):
        target = device(x, (y + 8 + ((place + 1) // 2) * (2 * (place % 2) - 1)) % 8, z2)
        remote(l_send.at[z2], l_recv.at[slot], target, 5, recv_sem.at[5])
        remote(o_send.at[z2, place], o_recv.at[slot], target, 4, recv_sem.at[4])

    def attend_group(offsets):
        for k in offsets:
            arrived(q_all.at[(z + k) % 8], qz_sem.at[(z + k) % 8])
        for k in offsets:
            attend((z + k) % 8)
        for k in offsets:
            z2 = (z + k) % 8
            loop(0, 7, lambda j: send_out(z2, 7 - j))
            if k:
                send_out(z2, 0)

    attend_group((0, 1, 7, 2))
    attend_group((6, 3, 5, 4))
    local(l_send.at[z], l_recv.at[slot], recv_sem.at[5])
    local(o_send.at[z, 0], o_recv.at[slot], recv_sem.at[4])

    arrived(l_recv, recv_sem.at[5])
    levels = l_recv[...].reshape(64, D)
    levels = jnp.transpose(jnp.concatenate([levels, levels], axis=0))
    apart = (y + 8 - lane % HEADS // 2) % 8
    place = jnp.where(apart <= 4, jnp.maximum(2 * apart - 1, 0), 16 - 2 * apart)
    mine = jnp.zeros((TOK, D), jnp.float32)
    for at in range(8):
        mine = jnp.where(place == at, levels[at * TOK:(at + 1) * TOK], mine)
    per_tower = [mine[:, t * HEADS:(t + 1) * HEADS] for t in range(3)]
    top = jnp.maximum(jnp.maximum(per_tower[0], per_tower[1]), per_tower[2])
    shares = [jnp.exp(level - top) for level in per_tower]
    share_sum = shares[0] + shares[1] + shares[2]
    shares = [share / share_sum for share in shares]
    arrived(o_recv, recv_sem.at[4])
    blocks = []
    squares = jnp.zeros((TOK, D), jnp.float32)
    for h in range(HEADS):
        block = o_recv[3 * HEADS + h].astype(jnp.float32)
        for t in range(3):
            block += shares[t][:, h:h + 1] * o_recv[t * HEADS + h].astype(jnp.float32)
        block = jnp.where(own_valid, block, 0.0).astype(jnp.bfloat16).astype(jnp.float32)
        blocks.append(block)
        squares += block * block
    mean = jnp.sum(squares, axis=1, keepdims=True) * (1.0 / (HEADS * D))
    norm = lax.rsqrt(mean + 1e-06)
    for h in range(HEADS):
        normed[h] = (blocks[h] * norm).astype(jnp.bfloat16)

    half_heads = HEADS // 2
    remote(normed.at[pl.ds((1 - cfg) * half_heads, half_heads)], paired, {"cfg": 1 - cfg}, 6, recv_sem.at[6])
    arrived(paired, recv_sem.at[6])
    for h in range(half_heads):
        here = normed[cfg * half_heads + h].astype(jnp.float32)
        there = paired[h].astype(jnp.float32)
        conditional = jnp.where(cfg == 0, here, there)
        unconditional = jnp.where(cfg == 0, there, here)
        guided = unconditional + guide[0] * (conditional - unconditional)
        out_ref[:, h * D:(h + 1) * D] = guided.astype(jnp.bfloat16)

    sent(kv_send.at[pl.ds(0, 15)], 0)
    sent(q_y.at[pl.ds(0, 7)], 1)
    sent(kv_all.at[pl.ds(0, 3)], 2)
    sent(q_all.at[pl.ds(0, 7)], 3)
    sent(o_recv.at[pl.ds(0, 63)], 4)
    sent(l_recv.at[pl.ds(0, 63)], 5)
    sent(paired, 6)


def per_device(query_self, query_cross, key_vectors, values, positions, counts, guidance):
    anywhere = pl.BlockSpec(memory_space=pltpu.HBM)
    bf16 = jnp.bfloat16
    return pl.pallas_call(
        kernel,
        out_shape=jax.ShapeDtypeStruct((TOK, HEADS * D // 2), bf16),
        in_specs=[anywhere] * 7,
        out_specs=pl.BlockSpec(memory_space=pltpu.VMEM),
        scratch_shapes=[
            pltpu.VMEM((4, TOK, HEADS * D), bf16),
            pltpu.SMEM((TOK,), jnp.int32),
            pltpu.SMEM((256,), jnp.int32),
            pltpu.SMEM((1,), jnp.float32),
            pltpu.VMEM((64, TOK, D), bf16),
            pltpu.VMEM((HEADS, 2, TOK, D), bf16),
            pltpu.VMEM((4, HEADS, 2, TOK, D), bf16),
            pltpu.VMEM((8, 2, 2, TOK, D), bf16),
            pltpu.VMEM((8, 2, 2, TOK, D), bf16),
            pltpu.VMEM((8, 8, TOK, D), bf16),
            pltpu.VMEM((D, 64 * TOK), bf16),
            pltpu.VMEM((8, 8, TOK, D), bf16),
            pltpu.VMEM((64, TOK, D), bf16),
            pltpu.VMEM((8, 1, D), jnp.float32),
            pltpu.VMEM((64, 1, D), jnp.float32),
            pltpu.VMEM((HEADS, TOK, D), bf16),
            pltpu.VMEM((HEADS // 2, TOK, D), bf16),
            pltpu.SemaphoreType.DMA((7,)),
            pltpu.SemaphoreType.DMA((7,)),
            pltpu.SemaphoreType.DMA((7,)),
            pltpu.SemaphoreType.DMA((16,)),
            pltpu.SemaphoreType.DMA((8,)),
            pltpu.SemaphoreType.DMA((8,)),
        ],
        compiler_params=pltpu.CompilerParams(
            collective_id=0, has_side_effects=True, vmem_limit_bytes=56 * 1024 * 1024
        ),
        name="twin_attention",
    )(query_self[0], query_cross[0], key_vectors[0], values[0], positions, counts, guidance)


def solution(mesh):
    return jax.shard_map(
        per_device,
        mesh=mesh,
        in_specs=(
            P("cfg", ("tower", "seq"), None),
            P("cfg", ("tower", "seq"), None),
            P("cfg", ("tower", "seq"), None),
            P("cfg", ("tower", "seq"), None),
            P(("tower", "seq")),
            P(),
            P(),
        ),
        out_specs=P(("tower", "seq"), "cfg"),
        check_vma=False,
    )
```

```python
import math

import jax
import jax.numpy as jnp
from jax import lax
from jax.experimental import pallas as pl
from jax.experimental.pallas import tpu as pltpu
from jax.sharding import PartitionSpec as P

HEADS = 16
D = 128
TOK = 16
SCALE = 1.0 / math.sqrt(D)
NEAR = (0, 1, 7, 2, 6, 3, 5, 4)
MESH = pl.DeviceIdType.MESH


def loop(lo, hi, fn):
    def body(k, carry):
        fn(k)
        return carry

    lax.fori_loop(lo, hi, body, 0)


def device(x, y, z):
    return {"tower": z // 2, "seq": (z % 2) * 32 + x * 8 + y}


def kernel(
    qs_hbm, qc_hbm, k_hbm, v_hbm, pos_hbm, counts_hbm,
    out_ref,
    raw, pos, counts, ones,
    kv_send, kv_all, q_rot, q_y, q_all, keys_t, o_send, o_recv, l_send, l_recv, normed, paired,
    load_sem, send_sem, recv_sem, kv_sem, qy_sem, qz_sem,
):
    cfg = lax.axis_index("cfg")
    tower = lax.axis_index("tower")
    seq = lax.axis_index("seq")
    zl, x, y = seq // 32, (seq // 8) % 4, seq % 8
    z = tower * 2 + zl

    def lo_peer(k):
        return (y + k // 2) % 8, (zl + k % 2) % 2

    def signal(target):
        pl.semaphore_signal(barrier, inc=1, device_id=target, device_id_type=MESH)

    def remote(src, dst, target, stage, landed):
        pltpu.make_async_remote_copy(
            src_ref=src, dst_ref=dst,
            send_sem=send_sem.at[stage], recv_sem=landed,
            device_id=target, device_id_type=MESH,
        ).start()

    def local(src, dst, landed):
        pltpu.make_async_copy(src, dst, landed).start()

    def arrived(like, landed):
        pltpu.make_async_copy(like, like, landed).wait()

    def sent(like, stage):
        pltpu.make_async_copy(like, like, send_sem.at[stage]).wait()

    barrier = pltpu.get_barrier_semaphore()

    def greet_lo(k):
        y2, zl2 = lo_peer(k)
        signal(device(x, y2, tower * 2 + zl2))

    loop(1, 16, greet_lo)
    loop(1, 8, lambda k: signal(device(x, y, (z + k) % 8)))
    loop(1, 4, lambda k: signal(device((x + k) % 4, y, z)))
    signal({"cfg": 1 - cfg})

    loads = [
        pltpu.make_async_copy(pos_hbm, pos, load_sem.at[4]),
        pltpu.make_async_copy(counts_hbm, counts, load_sem.at[5]),
        pltpu.make_async_copy(k_hbm, raw.at[2], load_sem.at[2]),
        pltpu.make_async_copy(v_hbm, raw.at[3], load_sem.at[3]),
        pltpu.make_async_copy(qs_hbm, raw.at[0], load_sem.at[0]),
        pltpu.make_async_copy(qc_hbm, raw.at[1], load_sem.at[1]),
    ]
    for copy in loads:
        copy.start()
    for copy in loads:
        copy.wait()

    row = lax.broadcasted_iota(jnp.int32, (TOK, D), 0)
    lane = lax.broadcasted_iota(jnp.int32, (TOK, D), 1)
    time = jnp.zeros((TOK, D), jnp.int32)
    for i in range(TOK):
        time = jnp.where(row == i, pos[i], time)
    half = (lane % 64).astype(jnp.float32)
    frequency = jnp.exp(half * (-2.0 / D * math.log(10000.0)))
    angle = time.astype(jnp.float32) * frequency
    cosine = jnp.cos(angle)
    sine = jnp.where(lane < 64, -jnp.sin(angle), jnp.sin(angle))

    def rope(which, h):
        block = raw[which, :, h * D:(h + 1) * D].astype(jnp.float32)
        return block * cosine + pltpu.roll(block, 64, axis=1) * sine

    own_valid = row < counts[tower * 64 + seq]
    for h in range(HEADS):
        keys = rope(2, h)
        kv_send[h, 0] = jnp.where(own_valid, keys, keys[0:1, :]).astype(jnp.bfloat16)
        vals = raw[3, :, h * D:(h + 1) * D]
        kv_send[h, 1] = jnp.where(own_valid, vals.astype(jnp.float32), 0.0).astype(jnp.bfloat16)
    for h in range(HEADS):
        q_rot[h // 2, 0, h % 2] = rope(0, h).astype(jnp.bfloat16)
        q_rot[h // 2, 1, h % 2] = rope(1, h).astype(jnp.bfloat16)

    pl.semaphore_wait(barrier, 15 + 7 + 3 + 1)

    own_slot = y * 2 + zl

    def send_kv(y2, zl2):
        remote(
            kv_send.at[y2 * 2 + zl2], kv_all.at[x, own_slot],
            device(x, y2, tower * 2 + zl2), 0, kv_sem.at[own_slot],
        )

    def send_q(k):
        place = NEAR.index((8 - k) % 8)
        remote(q_rot.at[(y + k) % 8], q_y.at[place], device(x, (y + k) % 8, z), 1, qy_sem.at[place])

    def pass_kv(pair):
        for k in (2, 1, 3):
            remote(pair, pair, device((x + k) % 4, y, z), 2, recv_sem.at[2])

    def q_for(z2, places):
        return q_y.at[places, (z // 6 + z2 // 6) % 2, z2 % 2]

    def pass_q(first, count):
        places = pl.ds(first, count)

        def pass_one(j):
            z2 = (z + (j + 3) % 7 + 1) % 8
            remote(q_for(z2, places), q_all.at[z, places], device(x, y, z2), 3, qz_sem.at[z])

        loop(0, 7, pass_one)
        local(q_for(z, places), q_all.at[z, places], qz_sem.at[z])

    local(q_rot.at[y], q_y.at[0], qy_sem.at[0])
    for k in (4, 3, 5, 2, 6, 1, 7):
        send_kv((y + k) % 8, zl)
        send_kv((y + k) % 8, 1 - zl)
    send_kv(y, 1 - zl)
    for k in (4, 3, 5, 2, 6, 1, 7):
        send_q(k)
    local(kv_send.at[own_slot], kv_all.at[x, own_slot], kv_sem.at[own_slot])

    def flags(i):
        count = counts[tower * 64 + (i % 2) * 32 + (i // 16) * 8 + (i // 2) % 8]
        ones[i] = jnp.where(row < count, 1.0, 0.0).astype(jnp.bfloat16)

    loop(0, 64, flags)

    arrived(kv_all.at[x, own_slot], kv_sem.at[own_slot])
    arrived(q_y.at[0], qy_sem.at[0])
    for place in range(8):
        y2 = (y + NEAR[place]) % 8
        pair = kv_all.at[x, pl.ds(2 * y2, 2)]
        for zl2 in range(2) if place else ():
            arrived(kv_all.at[x, 2 * y2 + zl2], kv_sem.at[2 * y2 + zl2])
        if place == 0:
            arrived(kv_all.at[x, y * 2 + 1 - zl], kv_sem.at[y * 2 + 1 - zl])
        pass_kv(pair)
    for place in range(1, 8):
        arrived(q_y.at[place], qy_sem.at[place])
    pass_q(0, 8)
    arrived(kv_all.at[pl.ds(0, 3)], recv_sem.at[2])

    slot = tower * HEADS + own_slot
    keys_t[...] = jnp.transpose(kv_all[:, :, 0].reshape(64 * TOK, D))

    def attend(z2):
        queries = q_all[z2].reshape(8 * TOK, D)
        values = jnp.concatenate(
            [kv_all[:, :, 1].reshape(64 * TOK, D), ones[...].reshape(64 * TOK, D)], axis=1
        )
        scores = jnp.dot(queries, keys_t[...], preferred_element_type=jnp.float32)
        highest = jnp.max(scores, axis=1, keepdims=True)
        weights = jnp.exp2((scores - highest) * (SCALE / math.log(2.0))).astype(jnp.bfloat16)
        total = jnp.dot(weights, values, preferred_element_type=jnp.float32)
        weight_sum = total[:, D:]
        o_send[z2] = (total[:, :D] / weight_sum).astype(jnp.bfloat16).reshape(8, TOK, D)
        level = highest * SCALE + jnp.log(weight_sum)
        l_send[z2] = jnp.transpose(level)[0:1, :]

    def send_out(z2, place):
        target = device(x, (y + 8 + ((place + 1) // 2) * (2 * (place % 2) - 1)) % 8, z2)
        remote(l_send.at[z2], l_recv.at[slot], target, 5, recv_sem.at[5])
        remote(o_send.at[z2, place], o_recv.at[slot], target, 4, recv_sem.at[4])

    def attend_group(offsets):
        for k in offsets:
            arrived(q_all.at[(z + k) % 8], qz_sem.at[(z + k) % 8])
        for k in offsets:
            attend((z + k) % 8)
        for k in offsets:
            z2 = (z + k) % 8
            loop(0, 7, lambda j: send_out(z2, 7 - j))
            if k:
                send_out(z2, 0)

    attend_group((4, 5, 3, 6))
    attend_group((2, 7, 1, 0))
    local(l_send.at[z], l_recv.at[slot], recv_sem.at[5])
    local(o_send.at[z, 0], o_recv.at[slot], recv_sem.at[4])

    arrived(l_recv, recv_sem.at[5])
    levels = l_recv[...].reshape(64, D)
    levels = jnp.transpose(jnp.concatenate([levels, levels], axis=0))
    apart = (y + 8 - lane % HEADS // 2) % 8
    place = jnp.where(apart <= 4, jnp.maximum(2 * apart - 1, 0), 16 - 2 * apart)
    mine = jnp.zeros((TOK, D), jnp.float32)
    for at in range(8):
        mine = jnp.where(place == at, levels[at * TOK:(at + 1) * TOK], mine)
    per_tower = [mine[:, t * HEADS:(t + 1) * HEADS] for t in range(3)]
    top = jnp.maximum(jnp.maximum(per_tower[0], per_tower[1]), per_tower[2])
    shares = [jnp.exp(level - top) for level in per_tower]
    share_sum = shares[0] + shares[1] + shares[2]
    shares = [share / share_sum for share in shares]
    arrived(o_recv, recv_sem.at[4])
    blocks = []
    squares = jnp.zeros((TOK, D), jnp.float32)
    for h in range(HEADS):
        block = o_recv[3 * HEADS + h].astype(jnp.float32)
        for t in range(3):
            block += shares[t][:, h:h + 1] * o_recv[t * HEADS + h].astype(jnp.float32)
        block = jnp.where(own_valid, block, 0.0).astype(jnp.bfloat16).astype(jnp.float32)
        blocks.append(block)
        squares += block * block
    mean = jnp.sum(squares, axis=1, keepdims=True) * (1.0 / (HEADS * D))
    norm = lax.rsqrt(mean + 1e-06)
    for h in range(HEADS):
        normed[h] = (blocks[h] * norm).astype(jnp.bfloat16)

    half_heads = HEADS // 2
    remote(normed.at[pl.ds((1 - cfg) * half_heads, half_heads)], paired, {"cfg": 1 - cfg}, 6, recv_sem.at[6])
    arrived(paired, recv_sem.at[6])
    for h in range(half_heads):
        here = normed[cfg * half_heads + h]
        out_ref[cfg, :, h * D:(h + 1) * D] = here
        out_ref[1 - cfg, :, h * D:(h + 1) * D] = paired[h]

    sent(kv_send.at[pl.ds(0, 15)], 0)
    sent(q_y.at[pl.ds(0, 7)], 1)
    sent(kv_all.at[pl.ds(0, 3)], 2)
    sent(q_all.at[pl.ds(0, 7)], 3)
    sent(o_recv.at[pl.ds(0, 63)], 4)
    sent(l_recv.at[pl.ds(0, 63)], 5)
    sent(paired, 6)


def per_device(query_self, query_cross, key_vectors, values, positions, counts, guidance):
    anywhere = pl.BlockSpec(memory_space=pltpu.HBM)
    bf16 = jnp.bfloat16
    both = pl.pallas_call(
        kernel,
        out_shape=jax.ShapeDtypeStruct((2, TOK, HEADS * D // 2), bf16),
        in_specs=[anywhere] * 6,
        out_specs=pl.BlockSpec(memory_space=pltpu.VMEM),
        scratch_shapes=[
            pltpu.VMEM((4, TOK, HEADS * D), bf16),
            pltpu.SMEM((TOK,), jnp.int32),
            pltpu.SMEM((256,), jnp.int32),
            pltpu.VMEM((64, TOK, D), bf16),
            pltpu.VMEM((HEADS, 2, TOK, D), bf16),
            pltpu.VMEM((4, HEADS, 2, TOK, D), bf16),
            pltpu.VMEM((8, 2, 2, TOK, D), bf16),
            pltpu.VMEM((8, 2, 2, TOK, D), bf16),
            pltpu.VMEM((8, 8, TOK, D), bf16),
            pltpu.VMEM((D, 64 * TOK), bf16),
            pltpu.VMEM((8, 8, TOK, D), bf16),
            pltpu.VMEM((64, TOK, D), bf16),
            pltpu.VMEM((8, 1, D), jnp.float32),
            pltpu.VMEM((64, 1, D), jnp.float32),
            pltpu.VMEM((HEADS, TOK, D), bf16),
            pltpu.VMEM((HEADS // 2, TOK, D), bf16),
            pltpu.SemaphoreType.DMA((7,)),
            pltpu.SemaphoreType.DMA((7,)),
            pltpu.SemaphoreType.DMA((7,)),
            pltpu.SemaphoreType.DMA((16,)),
            pltpu.SemaphoreType.DMA((8,)),
            pltpu.SemaphoreType.DMA((8,)),
        ],
        compiler_params=pltpu.CompilerParams(
            collective_id=0, has_side_effects=True, vmem_limit_bytes=56 * 1024 * 1024
        ),
        name="twin_attention",
    )(query_self[0], query_cross[0], key_vectors[0], values[0], positions, counts)
    conditional = both[0].astype(jnp.float32)
    unconditional = both[1].astype(jnp.float32)
    return (unconditional + guidance * (conditional - unconditional)).astype(bf16)


def solution(mesh):
    return jax.shard_map(
        per_device,
        mesh=mesh,
        in_specs=(
            P("cfg", ("tower", "seq"), None),
            P("cfg", ("tower", "seq"), None),
            P("cfg", ("tower", "seq"), None),
            P("cfg", ("tower", "seq"), None),
            P(("tower", "seq")),
            P(),
            P(),
        ),
        out_specs=P(("tower", "seq"), "cfg"),
        check_vma=False,
    )
```

```python
import math

import jax
import jax.numpy as jnp
from jax import lax
from jax.experimental import pallas as pl
from jax.experimental.pallas import tpu as pltpu
from jax.sharding import PartitionSpec as P

HEADS = 16
D = 128
TOK = 16
SCALE = 1.0 / math.sqrt(D)
NEAR = (0, 1, 7, 2, 6, 3, 5, 4)
MESH = pl.DeviceIdType.MESH


def loop(lo, hi, fn):
    def body(k, carry):
        fn(k)
        return carry

    lax.fori_loop(lo, hi, body, 0)


def device(x, y, z):
    return {"tower": z // 2, "seq": (z % 2) * 32 + x * 8 + y}


def kernel(
    qs_hbm, qc_hbm, k_hbm, v_hbm, pos_hbm, counts_hbm,
    out_ref,
    raw, pos, counts, ones,
    kv_send, kv_all, q_rot, q_y, q_all, keys_t, o_send, o_recv, l_send, l_recv, normed, paired,
    load_sem, send_sem, recv_sem, kv_sem, qy_sem, qz_sem,
):
    cfg = lax.axis_index("cfg")
    tower = lax.axis_index("tower")
    seq = lax.axis_index("seq")
    zl, x, y = seq // 32, (seq // 8) % 4, seq % 8
    z = tower * 2 + zl

    def signal(target):
        pl.semaphore_signal(barrier, inc=1, device_id=target, device_id_type=MESH)

    def remote(src, dst, target, stage, landed):
        pltpu.make_async_remote_copy(
            src_ref=src, dst_ref=dst,
            send_sem=send_sem.at[stage], recv_sem=landed,
            device_id=target, device_id_type=MESH,
        ).start()

    def local(src, dst, landed):
        pltpu.make_async_copy(src, dst, landed).start()

    def arrived(like, landed):
        pltpu.make_async_copy(like, like, landed).wait()

    def sent(like, stage):
        pltpu.make_async_copy(like, like, send_sem.at[stage]).wait()

    barrier = pltpu.get_barrier_semaphore()

    for k in (4, 3, 5, 2, 6, 1, 7):
        signal(device(x, (y + k) % 8, tower * 2 + 1 - zl))
    for k in (4, 3, 5, 2, 6, 1, 7):
        signal(device(x, (y + k) % 8, z))
        signal(device(x, y, (z + k) % 8))
    for k in (2, 1, 3):
        signal(device((x + k) % 4, y, z))
    signal({"cfg": 1 - cfg})

    loads = [
        pltpu.make_async_copy(pos_hbm, pos, load_sem.at[4]),
        pltpu.make_async_copy(counts_hbm, counts, load_sem.at[5]),
        pltpu.make_async_copy(k_hbm, raw.at[2], load_sem.at[2]),
        pltpu.make_async_copy(v_hbm, raw.at[3], load_sem.at[3]),
        pltpu.make_async_copy(qs_hbm, raw.at[0], load_sem.at[0]),
        pltpu.make_async_copy(qc_hbm, raw.at[1], load_sem.at[1]),
    ]
    for copy in loads:
        copy.start()
    for copy in loads:
        copy.wait()

    row = lax.broadcasted_iota(jnp.int32, (TOK, D), 0)
    lane = lax.broadcasted_iota(jnp.int32, (TOK, D), 1)
    time = jnp.zeros((TOK, D), jnp.int32)
    for i in range(TOK):
        time = jnp.where(row == i, pos[i], time)
    half = (lane % 64).astype(jnp.float32)
    frequency = jnp.exp(half * (-2.0 / D * math.log(10000.0)))
    angle = time.astype(jnp.float32) * frequency
    cosine = jnp.cos(angle)
    sine = jnp.where(lane < 64, -jnp.sin(angle), jnp.sin(angle))

    def rope(which, h):
        block = raw[which, :, h * D:(h + 1) * D].astype(jnp.float32)
        return block * cosine + pltpu.roll(block, 64, axis=1) * sine

    own_valid = row < counts[tower * 64 + seq]
    for h in range(HEADS):
        keys = rope(2, h)
        kv_send[h, 0] = jnp.where(own_valid, keys, keys[0:1, :]).astype(jnp.bfloat16)
        vals = raw[3, :, h * D:(h + 1) * D]
        kv_send[h, 1] = jnp.where(own_valid, vals.astype(jnp.float32), 0.0).astype(jnp.bfloat16)
    for h in range(HEADS):
        q_rot[h // 2, 0, h % 2] = rope(0, h).astype(jnp.bfloat16)
        q_rot[h // 2, 1, h % 2] = rope(1, h).astype(jnp.bfloat16)

    pl.semaphore_wait(barrier, 7 + 7 + 7 + 3 + 1)

    own_slot = y * 2 + zl

    def send_kv(y2, zl2):
        remote(
            kv_send.at[y2 * 2 + zl2], kv_all.at[x, own_slot],
            device(x, y2, tower * 2 + zl2), 0, kv_sem.at[own_slot],
        )

    def send_q(k):
        place = NEAR.index((8 - k) % 8)
        remote(q_rot.at[(y + k) % 8], q_y.at[place], device(x, (y + k) % 8, z), 1, qy_sem.at[place])

    def pass_kv(pair):
        for k in (2, 1, 3):
            remote(pair, pair, device((x + k) % 4, y, z), 2, recv_sem.at[2])

    def q_for(z2, places):
        return q_y.at[places, (z // 6 + z2 // 6) % 2, z2 % 2]

    def pass_q(first, count):
        places = pl.ds(first, count)

        for k in (4, 3, 5, 2, 6, 1, 7):
            z2 = (z + k) % 8
            remote(q_for(z2, places), q_all.at[z, places], device(x, y, z2), 3, qz_sem.at[z])

        local(q_for(z, places), q_all.at[z, places], qz_sem.at[z])

    local(q_rot.at[y], q_y.at[0], qy_sem.at[0])
    for k in (4, 3, 5, 2, 6, 1, 7):
        send_kv((y + k) % 8, zl)
        send_kv((y + k) % 8, 1 - zl)
    send_kv(y, 1 - zl)
    for k in (4, 3, 5, 2, 6, 1, 7):
        send_q(k)
    local(kv_send.at[own_slot], kv_all.at[x, own_slot], kv_sem.at[own_slot])

    def flags(i):
        count = counts[tower * 64 + (i % 2) * 32 + (i // 16) * 8 + (i // 2) % 8]
        ones[i] = jnp.where(row < count, 1.0, 0.0).astype(jnp.bfloat16)

    arrived(kv_all.at[x, own_slot], kv_sem.at[own_slot])
    arrived(q_y.at[0], qy_sem.at[0])
    for place in range(8):
        y2 = (y + NEAR[place]) % 8
        pair = kv_all.at[x, pl.ds(2 * y2, 2)]
        for zl2 in range(2) if place else ():
            arrived(kv_all.at[x, 2 * y2 + zl2], kv_sem.at[2 * y2 + zl2])
        if place == 0:
            arrived(kv_all.at[x, y * 2 + 1 - zl], kv_sem.at[y * 2 + 1 - zl])
        pass_kv(pair)
    for place in range(1, 8):
        arrived(q_y.at[place], qy_sem.at[place])
    pass_q(0, 8)
    loop(0, 64, flags)
    arrived(kv_all.at[pl.ds(0, 3)], recv_sem.at[2])

    slot = tower * HEADS + own_slot
    keys_t[...] = jnp.transpose(kv_all[:, :, 0].reshape(64 * TOK, D))

    def attend(z2):
        queries = q_all[z2].reshape(8 * TOK, D)
        values = jnp.concatenate(
            [kv_all[:, :, 1].reshape(64 * TOK, D), ones[...].reshape(64 * TOK, D)], axis=1
        )
        scores = jnp.dot(queries, keys_t[...], preferred_element_type=jnp.float32)
        highest = jnp.max(scores, axis=1, keepdims=True)
        weights = jnp.exp2((scores - highest) * (SCALE / math.log(2.0))).astype(jnp.bfloat16)
        total = jnp.dot(weights, values, preferred_element_type=jnp.float32)
        weight_sum = total[:, D:]
        o_send[z2] = (total[:, :D] / weight_sum).astype(jnp.bfloat16).reshape(8, TOK, D)
        level = highest * SCALE + jnp.log(weight_sum)
        l_send[z2] = jnp.transpose(level)[0:1, :]

    def send_out(z2, place):
        target = device(x, (y + NEAR[place]) % 8, z2)
        remote(l_send.at[z2], l_recv.at[slot], target, 5, recv_sem.at[5])
        remote(o_send.at[z2, place], o_recv.at[slot], target, 4, recv_sem.at[4])

    def attend_group(offsets):
        for k in offsets:
            arrived(q_all.at[(z + k) % 8], qz_sem.at[(z + k) % 8])
        for k in offsets:
            attend((z + k) % 8)
        for k in offsets:
            z2 = (z + k) % 8
            for place in range(7, -1 if k else 0, -1):
                send_out(z2, place)

    attend_group((4, 5, 3, 6))
    attend_group((2, 7, 1, 0))
    local(l_send.at[z], l_recv.at[slot], recv_sem.at[5])
    local(o_send.at[z, 0], o_recv.at[slot], recv_sem.at[4])

    arrived(l_recv, recv_sem.at[5])
    levels = l_recv[...].reshape(64, D)
    levels = jnp.transpose(jnp.concatenate([levels, levels], axis=0))
    apart = (y + 8 - lane % HEADS // 2) % 8
    place = jnp.where(apart <= 4, jnp.maximum(2 * apart - 1, 0), 16 - 2 * apart)
    mine = jnp.zeros((TOK, D), jnp.float32)
    for at in range(8):
        mine = jnp.where(place == at, levels[at * TOK:(at + 1) * TOK], mine)
    per_tower = [mine[:, t * HEADS:(t + 1) * HEADS] for t in range(3)]
    top = jnp.maximum(jnp.maximum(per_tower[0], per_tower[1]), per_tower[2])
    shares = [jnp.exp(level - top) for level in per_tower]
    share_sum = shares[0] + shares[1] + shares[2]
    shares = [share / share_sum for share in shares]
    arrived(o_recv, recv_sem.at[4])
    blocks = []
    squares = jnp.zeros((TOK, D), jnp.float32)
    for h in range(HEADS):
        block = o_recv[3 * HEADS + h].astype(jnp.float32)
        for t in range(3):
            block += shares[t][:, h:h + 1] * o_recv[t * HEADS + h].astype(jnp.float32)
        block = jnp.where(own_valid, block, 0.0).astype(jnp.bfloat16).astype(jnp.float32)
        blocks.append(block)
        squares += block * block
    mean = jnp.sum(squares, axis=1, keepdims=True) * (1.0 / (HEADS * D))
    norm = lax.rsqrt(mean + 1e-06)
    for h in range(HEADS):
        normed[h] = (blocks[h] * norm).astype(jnp.bfloat16)

    half_heads = HEADS // 2
    remote(normed.at[pl.ds((1 - cfg) * half_heads, half_heads)], paired, {"cfg": 1 - cfg}, 6, recv_sem.at[6])
    arrived(paired, recv_sem.at[6])
    for h in range(half_heads):
        here = normed[cfg * half_heads + h]
        out_ref[cfg, :, h * D:(h + 1) * D] = here
        out_ref[1 - cfg, :, h * D:(h + 1) * D] = paired[h]

    sent(kv_send.at[pl.ds(0, 15)], 0)
    sent(q_y.at[pl.ds(0, 7)], 1)
    sent(kv_all.at[pl.ds(0, 3)], 2)
    sent(q_all.at[pl.ds(0, 7)], 3)
    sent(o_recv.at[pl.ds(0, 63)], 4)
    sent(l_recv.at[pl.ds(0, 63)], 5)
    sent(paired, 6)


def per_device(query_self, query_cross, key_vectors, values, positions, counts, guidance):
    anywhere = pl.BlockSpec(memory_space=pltpu.HBM)
    bf16 = jnp.bfloat16
    both = pl.pallas_call(
        kernel,
        out_shape=jax.ShapeDtypeStruct((2, TOK, HEADS * D // 2), bf16),
        in_specs=[anywhere] * 6,
        out_specs=pl.BlockSpec(memory_space=pltpu.VMEM),
        scratch_shapes=[
            pltpu.VMEM((4, TOK, HEADS * D), bf16),
            pltpu.SMEM((TOK,), jnp.int32),
            pltpu.SMEM((256,), jnp.int32),
            pltpu.VMEM((64, TOK, D), bf16),
            pltpu.VMEM((HEADS, 2, TOK, D), bf16),
            pltpu.VMEM((4, HEADS, 2, TOK, D), bf16),
            pltpu.VMEM((8, 2, 2, TOK, D), bf16),
            pltpu.VMEM((8, 2, 2, TOK, D), bf16),
            pltpu.VMEM((8, 8, TOK, D), bf16),
            pltpu.VMEM((D, 64 * TOK), bf16),
            pltpu.VMEM((8, 8, TOK, D), bf16),
            pltpu.VMEM((64, TOK, D), bf16),
            pltpu.VMEM((8, 1, D), jnp.float32),
            pltpu.VMEM((64, 1, D), jnp.float32),
            pltpu.VMEM((HEADS, TOK, D), bf16),
            pltpu.VMEM((HEADS // 2, TOK, D), bf16),
            pltpu.SemaphoreType.DMA((7,)),
            pltpu.SemaphoreType.DMA((7,)),
            pltpu.SemaphoreType.DMA((7,)),
            pltpu.SemaphoreType.DMA((16,)),
            pltpu.SemaphoreType.DMA((8,)),
            pltpu.SemaphoreType.DMA((8,)),
        ],
        compiler_params=pltpu.CompilerParams(
            collective_id=0, has_side_effects=True, vmem_limit_bytes=56 * 1024 * 1024
        ),
        name="twin_attention",
    )(query_self[0], query_cross[0], key_vectors[0], values[0], positions, counts)
    conditional = both[0].astype(jnp.float32)
    unconditional = both[1].astype(jnp.float32)
    return (unconditional + guidance * (conditional - unconditional)).astype(bf16)


def solution(mesh):
    return jax.shard_map(
        per_device,
        mesh=mesh,
        in_specs=(
            P("cfg", ("tower", "seq"), None),
            P("cfg", ("tower", "seq"), None),
            P("cfg", ("tower", "seq"), None),
            P("cfg", ("tower", "seq"), None),
            P(("tower", "seq")),
            P(),
            P(),
        ),
        out_specs=P(("tower", "seq"), "cfg"),
        check_vma=False,
    )
```

```python
import math

import jax
import jax.numpy as jnp
from jax import lax
from jax.experimental import pallas as pl
from jax.experimental.pallas import tpu as pltpu
from jax.sharding import PartitionSpec as P

HEADS = 16
D = 128
TOK = 16
SCALE = 1.0 / math.sqrt(D)
NEAR = (0, 1, 7, 2, 6, 3, 5, 4)
MESH = pl.DeviceIdType.MESH


def loop(lo, hi, fn):
    def body(k, carry):
        fn(k)
        return carry

    lax.fori_loop(lo, hi, body, 0)


def device(x, y, z):
    return {"tower": z // 2, "seq": (z % 2) * 32 + x * 8 + y}


def kernel(
    qs_hbm, qc_hbm, k_hbm, v_hbm, pos_hbm, counts_hbm, guide_ref,
    out_ref,
    raw, pos, counts, ones,
    kv_send, kv_all, q_rot, q_y, q_all, keys_t, o_send, o_recv, l_send, l_recv, normed, paired,
    load_sem, send_sem, recv_sem, kv_sem, qy_sem, qz_sem,
):
    cfg = lax.axis_index("cfg")
    tower = lax.axis_index("tower")
    seq = lax.axis_index("seq")
    zl, x, y = seq // 32, (seq // 8) % 4, seq % 8
    z = tower * 2 + zl

    def signal(target):
        pl.semaphore_signal(barrier, inc=1, device_id=target, device_id_type=MESH)

    def remote(src, dst, target, stage, landed):
        pltpu.make_async_remote_copy(
            src_ref=src, dst_ref=dst,
            send_sem=send_sem.at[stage], recv_sem=landed,
            device_id=target, device_id_type=MESH,
        ).start()

    def local(src, dst, landed):
        pltpu.make_async_copy(src, dst, landed).start()

    def arrived(like, landed):
        pltpu.make_async_copy(like, like, landed).wait()

    def sent(like, stage):
        pltpu.make_async_copy(like, like, send_sem.at[stage]).wait()

    barrier = pltpu.get_barrier_semaphore()

    for k in (4, 3, 5, 2, 6, 1, 7):
        signal(device(x, (y + k) % 8, tower * 2 + 1 - zl))
    for k in (4, 3, 5, 2, 6, 1, 7):
        signal(device(x, (y + k) % 8, z))
        signal(device(x, y, (z + k) % 8))
    for k in (2, 1, 3):
        signal(device((x + k) % 4, y, z))
    signal({"cfg": 1 - cfg})

    loads = [
        pltpu.make_async_copy(pos_hbm, pos, load_sem.at[4]),
        pltpu.make_async_copy(counts_hbm, counts, load_sem.at[5]),
        pltpu.make_async_copy(k_hbm, raw.at[2], load_sem.at[2]),
        pltpu.make_async_copy(v_hbm, raw.at[3], load_sem.at[3]),
        pltpu.make_async_copy(qs_hbm, raw.at[0], load_sem.at[0]),
        pltpu.make_async_copy(qc_hbm, raw.at[1], load_sem.at[1]),
    ]
    for copy in loads:
        copy.start()
    for copy in loads:
        copy.wait()

    row = lax.broadcasted_iota(jnp.int32, (TOK, D), 0)
    lane = lax.broadcasted_iota(jnp.int32, (TOK, D), 1)
    time = jnp.zeros((TOK, D), jnp.int32)
    for i in range(TOK):
        time = jnp.where(row == i, pos[i], time)
    half = (lane % 64).astype(jnp.float32)
    frequency = jnp.exp(half * (-2.0 / D * math.log(10000.0)))
    angle = time.astype(jnp.float32) * frequency
    cosine = jnp.cos(angle)
    sine = jnp.where(lane < 64, -jnp.sin(angle), jnp.sin(angle))

    def rope(which, h):
        block = raw[which, :, h * D:(h + 1) * D].astype(jnp.float32)
        return block * cosine + pltpu.roll(block, 64, axis=1) * sine

    own_valid = row < counts[tower * 64 + seq]
    for h in range(HEADS):
        keys = rope(2, h)
        kv_send[h, 0] = jnp.where(own_valid, keys, keys[0:1, :]).astype(jnp.bfloat16)
        vals = raw[3, :, h * D:(h + 1) * D]
        kv_send[h, 1] = jnp.where(own_valid, vals.astype(jnp.float32), 0.0).astype(jnp.bfloat16)
    for h in range(HEADS):
        q_rot[h // 2, 0, h % 2] = rope(0, h).astype(jnp.bfloat16)
        q_rot[h // 2, 1, h % 2] = rope(1, h).astype(jnp.bfloat16)

    pl.semaphore_wait(barrier, 7 + 7 + 7 + 3 + 1)

    own_slot = y * 2 + zl

    def send_kv(y2, zl2):
        remote(
            kv_send.at[y2 * 2 + zl2], kv_all.at[x, own_slot],
            device(x, y2, tower * 2 + zl2), 0, kv_sem.at[own_slot],
        )

    def send_q(k):
        place = NEAR.index((8 - k) % 8)
        remote(q_rot.at[(y + k) % 8], q_y.at[place], device(x, (y + k) % 8, z), 1, qy_sem.at[place])

    def pass_kv(pair):
        for k in (2, 1, 3):
            remote(pair, pair, device((x + k) % 4, y, z), 2, recv_sem.at[2])

    def q_for(z2, places):
        return q_y.at[places, (z // 6 + z2 // 6) % 2, z2 % 2]

    def pass_q(first, count):
        places = pl.ds(first, count)

        for k in (4, 3, 5, 2, 6, 1, 7):
            z2 = (z + k) % 8
            remote(q_for(z2, places), q_all.at[z, places], device(x, y, z2), 3, qz_sem.at[z])

        local(q_for(z, places), q_all.at[z, places], qz_sem.at[z])

    local(q_rot.at[y], q_y.at[0], qy_sem.at[0])
    for k in (4, 3, 5, 2, 6, 1, 7):
        send_kv((y + k) % 8, zl)
        send_kv((y + k) % 8, 1 - zl)
    send_kv(y, 1 - zl)
    for k in (4, 3, 5, 2, 6, 1, 7):
        send_q(k)
    local(kv_send.at[own_slot], kv_all.at[x, own_slot], kv_sem.at[own_slot])

    def flags(i):
        count = counts[tower * 64 + (i % 2) * 32 + (i // 16) * 8 + (i // 2) % 8]
        ones[i] = jnp.where(row < count, 1.0, 0.0).astype(jnp.bfloat16)

    arrived(kv_all.at[x, own_slot], kv_sem.at[own_slot])
    arrived(q_y.at[0], qy_sem.at[0])
    for place in range(8):
        y2 = (y + NEAR[place]) % 8
        pair = kv_all.at[x, pl.ds(2 * y2, 2)]
        for zl2 in range(2) if place else ():
            arrived(kv_all.at[x, 2 * y2 + zl2], kv_sem.at[2 * y2 + zl2])
        if place == 0:
            arrived(kv_all.at[x, y * 2 + 1 - zl], kv_sem.at[y * 2 + 1 - zl])
        pass_kv(pair)
    for place in range(1, 8):
        arrived(q_y.at[place], qy_sem.at[place])
    pass_q(0, 8)
    loop(0, 64, flags)
    arrived(kv_all.at[pl.ds(0, 3)], recv_sem.at[2])

    slot = tower * HEADS + own_slot
    keys_t[...] = jnp.transpose(kv_all[:, :, 0].reshape(64 * TOK, D))

    def attend(z2):
        queries = q_all[z2].reshape(8 * TOK, D)
        values = jnp.concatenate(
            [kv_all[:, :, 1].reshape(64 * TOK, D), ones[...].reshape(64 * TOK, D)], axis=1
        )
        scores = jnp.dot(queries, keys_t[...], preferred_element_type=jnp.float32)
        highest = jnp.max(scores, axis=1, keepdims=True)
        weights = jnp.exp2((scores - highest) * (SCALE / math.log(2.0))).astype(jnp.bfloat16)
        total = jnp.dot(weights, values, preferred_element_type=jnp.float32)
        weight_sum = total[:, D:]
        o_send[z2] = (total[:, :D] / weight_sum).astype(jnp.bfloat16).reshape(8, TOK, D)
        level = highest * SCALE + jnp.log(weight_sum)
        l_send[z2] = jnp.transpose(level)[0:1, :]

    def send_out(z2, place):
        target = device(x, (y + NEAR[place]) % 8, z2)
        remote(l_send.at[z2], l_recv.at[slot], target, 5, recv_sem.at[5])
        remote(o_send.at[z2, place], o_recv.at[slot], target, 4, recv_sem.at[4])

    def attend_group(offsets):
        for k in offsets:
            arrived(q_all.at[(z + k) % 8], qz_sem.at[(z + k) % 8])
        for k in offsets:
            attend((z + k) % 8)
        for k in offsets:
            z2 = (z + k) % 8
            for place in range(7, -1 if k else 0, -1):
                send_out(z2, place)

    attend_group((4, 5, 3, 6))
    attend_group((2, 7, 1, 0))
    local(l_send.at[z], l_recv.at[slot], recv_sem.at[5])
    local(o_send.at[z, 0], o_recv.at[slot], recv_sem.at[4])

    arrived(l_recv, recv_sem.at[5])
    levels = l_recv[...].reshape(64, D)
    levels = jnp.transpose(jnp.concatenate([levels, levels], axis=0))
    apart = (y + 8 - lane % HEADS // 2) % 8
    place = jnp.where(apart <= 4, jnp.maximum(2 * apart - 1, 0), 16 - 2 * apart)
    mine = jnp.zeros((TOK, D), jnp.float32)
    for at in range(8):
        mine = jnp.where(place == at, levels[at * TOK:(at + 1) * TOK], mine)
    per_tower = [mine[:, t * HEADS:(t + 1) * HEADS] for t in range(3)]
    top = jnp.maximum(jnp.maximum(per_tower[0], per_tower[1]), per_tower[2])
    shares = [jnp.exp(level - top) for level in per_tower]
    share_sum = shares[0] + shares[1] + shares[2]
    shares = [share / share_sum for share in shares]
    arrived(o_recv, recv_sem.at[4])
    blocks = []
    squares = jnp.zeros((TOK, D), jnp.float32)
    for h in range(HEADS):
        block = o_recv[3 * HEADS + h].astype(jnp.float32)
        for t in range(3):
            block += shares[t][:, h:h + 1] * o_recv[t * HEADS + h].astype(jnp.float32)
        block = jnp.where(own_valid, block, 0.0).astype(jnp.bfloat16).astype(jnp.float32)
        blocks.append(block)
        squares += block * block
    mean = jnp.sum(squares, axis=1, keepdims=True) * (1.0 / (HEADS * D))
    norm = lax.rsqrt(mean + 1e-06)
    for h in range(HEADS):
        normed[h] = (blocks[h] * norm).astype(jnp.bfloat16)

    half_heads = HEADS // 2
    remote(normed.at[pl.ds((1 - cfg) * half_heads, half_heads)], paired, {"cfg": 1 - cfg}, 6, recv_sem.at[6])
    arrived(paired, recv_sem.at[6])
    for h in range(half_heads):
        here = normed[cfg * half_heads + h].astype(jnp.float32)
        there = paired[h].astype(jnp.float32)
        conditional = jnp.where(cfg == 0, here, there)
        unconditional = jnp.where(cfg == 0, there, here)
        guided = unconditional + guide_ref[0] * (conditional - unconditional)
        out_ref[:, h * D:(h + 1) * D] = guided.astype(jnp.bfloat16)

    sent(kv_send.at[pl.ds(0, 15)], 0)
    sent(q_y.at[pl.ds(0, 7)], 1)
    sent(kv_all.at[pl.ds(0, 3)], 2)
    sent(q_all.at[pl.ds(0, 7)], 3)
    sent(o_recv.at[pl.ds(0, 63)], 4)
    sent(l_recv.at[pl.ds(0, 63)], 5)
    sent(paired, 6)


def per_device(query_self, query_cross, key_vectors, values, positions, counts, guidance):
    anywhere = pl.BlockSpec(memory_space=pltpu.HBM)
    bf16 = jnp.bfloat16
    return pl.pallas_call(
        kernel,
        out_shape=pltpu.VMEM((TOK, HEADS * D // 2), bf16),
        in_specs=[anywhere] * 6 + [pl.BlockSpec(memory_space=pltpu.SMEM)],
        out_specs=pl.BlockSpec(memory_space=pltpu.VMEM),
        scratch_shapes=[
            pltpu.VMEM((4, TOK, HEADS * D), bf16),
            pltpu.SMEM((TOK,), jnp.int32),
            pltpu.SMEM((256,), jnp.int32),
            pltpu.VMEM((64, TOK, D), bf16),
            pltpu.VMEM((HEADS, 2, TOK, D), bf16),
            pltpu.VMEM((4, HEADS, 2, TOK, D), bf16),
            pltpu.VMEM((8, 2, 2, TOK, D), bf16),
            pltpu.VMEM((8, 2, 2, TOK, D), bf16),
            pltpu.VMEM((8, 8, TOK, D), bf16),
            pltpu.VMEM((D, 64 * TOK), bf16),
            pltpu.VMEM((8, 8, TOK, D), bf16),
            pltpu.VMEM((64, TOK, D), bf16),
            pltpu.VMEM((8, 1, D), jnp.float32),
            pltpu.VMEM((64, 1, D), jnp.float32),
            pltpu.VMEM((HEADS, TOK, D), bf16),
            pltpu.VMEM((HEADS // 2, TOK, D), bf16),
            pltpu.SemaphoreType.DMA((7,)),
            pltpu.SemaphoreType.DMA((7,)),
            pltpu.SemaphoreType.DMA((7,)),
            pltpu.SemaphoreType.DMA((16,)),
            pltpu.SemaphoreType.DMA((8,)),
            pltpu.SemaphoreType.DMA((8,)),
        ],
        compiler_params=pltpu.CompilerParams(
            collective_id=0, has_side_effects=True, vmem_limit_bytes=56 * 1024 * 1024
        ),
        name="twin_attention",
    )(query_self[0], query_cross[0], key_vectors[0], values[0], positions, counts, guidance)


def solution(mesh):
    return jax.shard_map(
        per_device,
        mesh=mesh,
        in_specs=(
            P("cfg", ("tower", "seq"), None),
            P("cfg", ("tower", "seq"), None),
            P("cfg", ("tower", "seq"), None),
            P("cfg", ("tower", "seq"), None),
            P(("tower", "seq")),
            P(),
            P(),
        ),
        out_specs=P(("tower", "seq"), "cfg"),
        check_vma=False,
    )
```

```python
import math

import jax
import jax.numpy as jnp
from jax import lax
from jax.experimental import pallas as pl
from jax.experimental.pallas import tpu as pltpu
from jax.sharding import PartitionSpec as P

HEADS = 16
D = 128
TOK = 16
SCALE = 1.0 / math.sqrt(D)
NEAR = (0, 1, 7, 2, 6, 3, 5, 4)
MESH = pl.DeviceIdType.MESH


def hops(dy, dz):
    return min(dy, 8 - dy) + min(dz, 8 - dz)


AROUND = sorted(
    ((dy, dz) for dy in range(8) for dz in range(8) if dy or dz), key=lambda d: (-hops(*d), d)
)
CLOSE = [d for d in AROUND if hops(*d) <= 5]
FAR = [d for d in AROUND if hops(*d) > 5]
FAR_DY = (2, 6, 3, 5, 4)
FAR_DZ = {dy: [dz for dy2, dz in FAR if dy2 == dy] for dy in FAR_DY}


def loop(lo, hi, fn):
    def body(k, carry):
        fn(k)
        return carry

    lax.fori_loop(lo, hi, body, 0)


def device(x, y, z):
    return {"tower": z // 2, "seq": (z % 2) * 32 + x * 8 + y}


def kernel(
    qs_hbm, qc_hbm, k_hbm, v_hbm, pos_hbm, counts_hbm, guide_ref,
    out_ref,
    raw, pos, counts, ones,
    kv_send, kv_all, q_rot, q_far, q_all, keys_t, o_send, o_recv, l_send, l_recv, normed, paired,
    load_sem, send_sem, recv_sem, kv_sem, qy_sem, qz_sem,
):
    cfg = lax.axis_index("cfg")
    tower = lax.axis_index("tower")
    seq = lax.axis_index("seq")
    zl, x, y = seq // 32, (seq // 8) % 4, seq % 8
    z = tower * 2 + zl

    def signal(target):
        pl.semaphore_signal(barrier, inc=1, device_id=target, device_id_type=MESH)

    def remote(src, dst, target, stage, landed):
        pltpu.make_async_remote_copy(
            src_ref=src, dst_ref=dst,
            send_sem=send_sem.at[stage], recv_sem=landed,
            device_id=target, device_id_type=MESH,
        ).start()

    def local(src, dst, landed):
        pltpu.make_async_copy(src, dst, landed).start()

    def arrived(like, landed):
        pltpu.make_async_copy(like, like, landed).wait()

    def sent(like, stage):
        pltpu.make_async_copy(like, like, send_sem.at[stage]).wait()

    barrier = pltpu.get_barrier_semaphore()

    for dy, dz in CLOSE:
        signal(device(x, (y + dy) % 8, (z + dz) % 8))
    for k in (2, 1, 3):
        signal(device((x + k) % 4, y, z))
    signal({"cfg": 1 - cfg})

    loads = [
        pltpu.make_async_copy(pos_hbm, pos, load_sem.at[4]),
        pltpu.make_async_copy(counts_hbm, counts, load_sem.at[5]),
        pltpu.make_async_copy(k_hbm, raw.at[2], load_sem.at[2]),
        pltpu.make_async_copy(v_hbm, raw.at[3], load_sem.at[3]),
        pltpu.make_async_copy(qs_hbm, raw.at[0], load_sem.at[0]),
        pltpu.make_async_copy(qc_hbm, raw.at[1], load_sem.at[1]),
    ]
    for copy in loads:
        copy.start()
    for copy in loads:
        copy.wait()

    row = lax.broadcasted_iota(jnp.int32, (TOK, D), 0)
    lane = lax.broadcasted_iota(jnp.int32, (TOK, D), 1)
    time = jnp.zeros((TOK, D), jnp.int32)
    for i in range(TOK):
        time = jnp.where(row == i, pos[i], time)
    half = (lane % 64).astype(jnp.float32)
    frequency = jnp.exp(half * (-2.0 / D * math.log(10000.0)))
    angle = time.astype(jnp.float32) * frequency
    cosine = jnp.cos(angle)
    sine = jnp.where(lane < 64, -jnp.sin(angle), jnp.sin(angle))

    def rope(which, h):
        block = raw[which, :, h * D:(h + 1) * D].astype(jnp.float32)
        return block * cosine + pltpu.roll(block, 64, axis=1) * sine

    own_valid = row < counts[tower * 64 + seq]
    for h in range(HEADS):
        keys = rope(2, h)
        kv_send[h, 0] = jnp.where(own_valid, keys, keys[0:1, :]).astype(jnp.bfloat16)
        vals = raw[3, :, h * D:(h + 1) * D]
        kv_send[h, 1] = jnp.where(own_valid, vals.astype(jnp.float32), 0.0).astype(jnp.bfloat16)
    for h in range(HEADS):
        q_rot[h // 2, 0, h % 2] = rope(0, h).astype(jnp.bfloat16)
        q_rot[h // 2, 1, h % 2] = rope(1, h).astype(jnp.bfloat16)

    pl.semaphore_wait(barrier, len(CLOSE) + 3 + 1)

    own_slot = y * 2 + zl

    def send_kv(y2, zl2):
        remote(
            kv_send.at[y2 * 2 + zl2], kv_all.at[x, own_slot],
            device(x, y2, tower * 2 + zl2), 0, kv_sem.at[own_slot],
        )

    def q_for(dy, z2):
        return q_rot.at[(y + dy) % 8, (z // 6 + z2 // 6) % 2, z2 % 2]

    def place_from(dy):
        return NEAR.index((8 - dy) % 8)

    def send_q(dy, dz):
        z2 = (z + dz) % 8
        block, target = q_all.at[z, place_from(dy)], device(x, (y + dy) % 8, z2)
        remote(q_for(dy, z2), block, target, 3, qz_sem.at[z])

    def send_far_q(dy, dz):
        block = q_far.at[FAR.index((dy, dz))]
        remote(q_for(dy, (z + dz) % 8), block, device(x, (y + dy) % 8, z), 1, qy_sem.at[dy])

    def pass_far_q(dy, dz):
        block = q_far.at[FAR.index((dy, dz))]
        target = device(x, y, (z + dz) % 8)
        remote(block, q_all.at[z, place_from(dy)], target, 3, qz_sem.at[z])

    def pass_kv(pair):
        for k in (2, 1, 3):
            remote(pair, pair, device((x + k) % 4, y, z), 2, recv_sem.at[2])

    for k in (4, 3, 5, 2, 6, 1, 7):
        send_kv((y + k) % 8, zl)
        send_kv((y + k) % 8, 1 - zl)
    send_kv(y, 1 - zl)
    for dy, dz in FAR:
        send_far_q(dy, dz)
    for dy, dz in CLOSE:
        send_q(dy, dz)
    local(q_for(0, z), q_all.at[z, 0], qz_sem.at[z])
    local(kv_send.at[own_slot], kv_all.at[x, own_slot], kv_sem.at[own_slot])

    def flags(i):
        count = counts[tower * 64 + (i % 2) * 32 + (i // 16) * 8 + (i // 2) % 8]
        ones[i] = jnp.where(row < count, 1.0, 0.0).astype(jnp.bfloat16)

    arrived(kv_all.at[x, own_slot], kv_sem.at[own_slot])
    for place in range(8):
        y2 = (y + NEAR[place]) % 8
        pair = kv_all.at[x, pl.ds(2 * y2, 2)]
        for zl2 in range(2) if place else ():
            arrived(kv_all.at[x, 2 * y2 + zl2], kv_sem.at[2 * y2 + zl2])
        if place == 0:
            arrived(kv_all.at[x, y * 2 + 1 - zl], kv_sem.at[y * 2 + 1 - zl])
        pass_kv(pair)
    for dy in FAR_DY:
        arrived(q_far.at[pl.ds(0, len(FAR_DZ[dy]))], qy_sem.at[dy])
        for dz in FAR_DZ[dy]:
            pass_far_q(dy, dz)
    loop(0, 64, flags)
    arrived(kv_all.at[pl.ds(0, 3)], recv_sem.at[2])

    slot = tower * HEADS + own_slot
    keys_t[...] = jnp.transpose(kv_all[:, :, 0].reshape(64 * TOK, D))

    def attend(z2):
        queries = q_all[z2].reshape(8 * TOK, D)
        values = jnp.concatenate(
            [kv_all[:, :, 1].reshape(64 * TOK, D), ones[...].reshape(64 * TOK, D)], axis=1
        )
        scores = jnp.dot(queries, keys_t[...], preferred_element_type=jnp.float32)
        highest = jnp.max(scores, axis=1, keepdims=True)
        weights = jnp.exp2((scores - highest) * (SCALE / math.log(2.0))).astype(jnp.bfloat16)
        total = jnp.dot(weights, values, preferred_element_type=jnp.float32)
        weight_sum = total[:, D:]
        o_send[z2] = (total[:, :D] / weight_sum).astype(jnp.bfloat16).reshape(8, TOK, D)
        level = highest * SCALE + jnp.log(weight_sum)
        l_send[z2] = jnp.transpose(level)[0:1, :]

    def send_out(z2, place):
        target = device(x, (y + NEAR[place]) % 8, z2)
        remote(l_send.at[z2], l_recv.at[slot], target, 5, recv_sem.at[5])
        remote(o_send.at[z2, place], o_recv.at[slot], target, 4, recv_sem.at[4])

    def attend_group(offsets):
        for k in offsets:
            arrived(q_all.at[(z + k) % 8], qz_sem.at[(z + k) % 8])
        for k in offsets:
            attend((z + k) % 8)
        for k in offsets:
            z2 = (z + k) % 8
            for place in range(7, -1 if k else 0, -1):
                send_out(z2, place)

    attend_group((4, 5, 3, 6))
    attend_group((2, 7, 1, 0))
    local(l_send.at[z], l_recv.at[slot], recv_sem.at[5])
    local(o_send.at[z, 0], o_recv.at[slot], recv_sem.at[4])

    arrived(l_recv, recv_sem.at[5])
    levels = l_recv[...].reshape(64, D)
    levels = jnp.transpose(jnp.concatenate([levels, levels], axis=0))
    apart = (y + 8 - lane % HEADS // 2) % 8
    place = jnp.where(apart <= 4, jnp.maximum(2 * apart - 1, 0), 16 - 2 * apart)
    mine = jnp.zeros((TOK, D), jnp.float32)
    for at in range(8):
        mine = jnp.where(place == at, levels[at * TOK:(at + 1) * TOK], mine)
    per_tower = [mine[:, t * HEADS:(t + 1) * HEADS] for t in range(3)]
    top = jnp.maximum(jnp.maximum(per_tower[0], per_tower[1]), per_tower[2])
    shares = [jnp.exp(level - top) for level in per_tower]
    share_sum = shares[0] + shares[1] + shares[2]
    shares = [share / share_sum for share in shares]
    arrived(o_recv, recv_sem.at[4])
    blocks = []
    squares = jnp.zeros((TOK, D), jnp.float32)
    for h in range(HEADS):
        block = o_recv[3 * HEADS + h].astype(jnp.float32)
        for t in range(3):
            block += shares[t][:, h:h + 1] * o_recv[t * HEADS + h].astype(jnp.float32)
        block = jnp.where(own_valid, block, 0.0).astype(jnp.bfloat16).astype(jnp.float32)
        blocks.append(block)
        squares += block * block
    mean = jnp.sum(squares, axis=1, keepdims=True) * (1.0 / (HEADS * D))
    norm = lax.rsqrt(mean + 1e-06)
    for h in range(HEADS):
        normed[h] = (blocks[h] * norm).astype(jnp.bfloat16)

    half_heads = HEADS // 2
    remote(normed.at[pl.ds((1 - cfg) * half_heads, half_heads)], paired, {"cfg": 1 - cfg}, 6, recv_sem.at[6])
    arrived(paired, recv_sem.at[6])
    for h in range(half_heads):
        here = normed[cfg * half_heads + h].astype(jnp.float32)
        there = paired[h].astype(jnp.float32)
        conditional = jnp.where(cfg == 0, here, there)
        unconditional = jnp.where(cfg == 0, there, here)
        guided = unconditional + guide_ref[0] * (conditional - unconditional)
        out_ref[:, h * D:(h + 1) * D] = guided.astype(jnp.bfloat16)

    sent(kv_send.at[pl.ds(0, 15)], 0)
    sent(q_far, 1)
    sent(kv_all.at[pl.ds(0, 3)], 2)
    sent(o_recv.at[pl.ds(0, 63)], 3)
    sent(o_recv.at[pl.ds(0, 63)], 4)
    sent(l_recv.at[pl.ds(0, 63)], 5)
    sent(paired, 6)


def per_device(query_self, query_cross, key_vectors, values, positions, counts, guidance):
    anywhere = pl.BlockSpec(memory_space=pltpu.HBM)
    bf16 = jnp.bfloat16
    return pl.pallas_call(
        kernel,
        out_shape=pltpu.VMEM((TOK, HEADS * D // 2), bf16),
        in_specs=[anywhere] * 6 + [pl.BlockSpec(memory_space=pltpu.SMEM)],
        out_specs=pl.BlockSpec(memory_space=pltpu.VMEM),
        scratch_shapes=[
            pltpu.VMEM((4, TOK, HEADS * D), bf16),
            pltpu.SMEM((TOK,), jnp.int32),
            pltpu.SMEM((256,), jnp.int32),
            pltpu.VMEM((64, TOK, D), bf16),
            pltpu.VMEM((HEADS, 2, TOK, D), bf16),
            pltpu.VMEM((4, HEADS, 2, TOK, D), bf16),
            pltpu.VMEM((8, 2, 2, TOK, D), bf16),
            pltpu.VMEM((len(FAR), TOK, D), bf16),
            pltpu.VMEM((8, 8, TOK, D), bf16),
            pltpu.VMEM((D, 64 * TOK), bf16),
            pltpu.VMEM((8, 8, TOK, D), bf16),
            pltpu.VMEM((64, TOK, D), bf16),
            pltpu.VMEM((8, 1, D), jnp.float32),
            pltpu.VMEM((64, 1, D), jnp.float32),
            pltpu.VMEM((HEADS, TOK, D), bf16),
            pltpu.VMEM((HEADS // 2, TOK, D), bf16),
            pltpu.SemaphoreType.DMA((7,)),
            pltpu.SemaphoreType.DMA((7,)),
            pltpu.SemaphoreType.DMA((7,)),
            pltpu.SemaphoreType.DMA((16,)),
            pltpu.SemaphoreType.DMA((8,)),
            pltpu.SemaphoreType.DMA((8,)),
        ],
        compiler_params=pltpu.CompilerParams(
            collective_id=0, has_side_effects=True, vmem_limit_bytes=56 * 1024 * 1024
        ),
        name="twin_attention",
    )(query_self[0], query_cross[0], key_vectors[0], values[0], positions, counts, guidance)


def solution(mesh):
    return jax.shard_map(
        per_device,
        mesh=mesh,
        in_specs=(
            P("cfg", ("tower", "seq"), None),
            P("cfg", ("tower", "seq"), None),
            P("cfg", ("tower", "seq"), None),
            P("cfg", ("tower", "seq"), None),
            P(("tower", "seq")),
            P(),
            P(),
        ),
        out_specs=P(("tower", "seq"), "cfg"),
        check_vma=False,
    )
```

```python
import math

import jax
import jax.numpy as jnp
from jax import lax
from jax.experimental import pallas as pl
from jax.experimental.pallas import tpu as pltpu
from jax.sharding import PartitionSpec as P

HEADS = 16
D = 128
TOK = 16
SCALE = 1.0 / math.sqrt(D)
NEAR = (0, 1, 7, 2, 6, 3, 5, 4)
MESH = pl.DeviceIdType.MESH


def hops(dy, dz):
    return min(dy, 8 - dy) + min(dz, 8 - dz)


AROUND = sorted(
    ((dy, dz) for dy in range(8) for dz in range(8) if dy or dz), key=lambda d: (-hops(*d), d)
)
CLOSE = [d for d in AROUND if hops(*d) <= 5]
FAR = [d for d in AROUND if hops(*d) > 5]
FAR_DY = (2, 6, 3, 5, 4)
FAR_DZ = {dy: [dz for dy2, dz in FAR if dy2 == dy] for dy in FAR_DY}


def loop(lo, hi, fn):
    def body(k, carry):
        fn(k)
        return carry

    lax.fori_loop(lo, hi, body, 0)


def device(x, y, z):
    return {"tower": z // 2, "seq": (z % 2) * 32 + x * 8 + y}


def kernel(
    qs_hbm, qc_hbm, k_hbm, v_hbm, pos_hbm, counts_hbm, guide_ref,
    out_ref,
    raw, pos, counts, ones,
    kv_send, kv_all, q_rot, q_far, q_all, keys_t, o_send, o_recv, l_send, l_recv, merged, paired, scale_here, scale_there,
    load_sem, send_sem, recv_sem, kv_sem, qy_sem, qz_sem,
):
    cfg = lax.axis_index("cfg")
    tower = lax.axis_index("tower")
    seq = lax.axis_index("seq")
    zl, x, y = seq // 32, (seq // 8) % 4, seq % 8
    z = tower * 2 + zl

    def signal(target):
        pl.semaphore_signal(barrier, inc=1, device_id=target, device_id_type=MESH)

    def remote(src, dst, target, stage, landed):
        pltpu.make_async_remote_copy(
            src_ref=src, dst_ref=dst,
            send_sem=send_sem.at[stage], recv_sem=landed,
            device_id=target, device_id_type=MESH,
        ).start()

    def local(src, dst, landed):
        pltpu.make_async_copy(src, dst, landed).start()

    def arrived(like, landed):
        pltpu.make_async_copy(like, like, landed).wait()

    def sent(like, stage):
        pltpu.make_async_copy(like, like, send_sem.at[stage]).wait()

    loads = [
        pltpu.make_async_copy(pos_hbm, pos, load_sem.at[4]),
        pltpu.make_async_copy(counts_hbm, counts, load_sem.at[5]),
        pltpu.make_async_copy(k_hbm, raw.at[2], load_sem.at[2]),
        pltpu.make_async_copy(v_hbm, raw.at[3], load_sem.at[3]),
        pltpu.make_async_copy(qs_hbm, raw.at[0], load_sem.at[0]),
        pltpu.make_async_copy(qc_hbm, raw.at[1], load_sem.at[1]),
    ]
    for copy in loads:
        copy.start()

    barrier = pltpu.get_barrier_semaphore()

    for dy, dz in CLOSE:
        signal(device(x, (y + dy) % 8, (z + dz) % 8))
    for k in (2, 1, 3):
        signal(device((x + k) % 4, y, z))
    signal({"cfg": 1 - cfg})

    for copy in loads:
        copy.wait()

    row = lax.broadcasted_iota(jnp.int32, (TOK, D), 0)
    lane = lax.broadcasted_iota(jnp.int32, (TOK, D), 1)
    time = jnp.zeros((TOK, D), jnp.int32)
    for i in range(TOK):
        time = jnp.where(row == i, pos[i], time)
    half = (lane % 64).astype(jnp.float32)
    frequency = jnp.exp(half * (-2.0 / D * math.log(10000.0)))
    angle = time.astype(jnp.float32) * frequency
    cosine = jnp.cos(angle)
    sine = jnp.where(lane < 64, -jnp.sin(angle), jnp.sin(angle))

    def rope(which, h):
        block = raw[which, :, h * D:(h + 1) * D].astype(jnp.float32)
        return block * cosine + pltpu.roll(block, 64, axis=1) * sine

    own_valid = row < counts[tower * 64 + seq]
    for h in range(HEADS):
        keys = rope(2, h)
        kv_send[h, 0] = jnp.where(own_valid, keys, keys[0:1, :]).astype(jnp.bfloat16)
        vals = raw[3, :, h * D:(h + 1) * D]
        kv_send[h, 1] = jnp.where(own_valid, vals.astype(jnp.float32), 0.0).astype(jnp.bfloat16)
    for h in range(HEADS):
        q_rot[h // 2, 0, h % 2] = rope(0, h).astype(jnp.bfloat16)
        q_rot[h // 2, 1, h % 2] = rope(1, h).astype(jnp.bfloat16)

    pl.semaphore_wait(barrier, len(CLOSE) + 3 + 1)

    own_slot = y * 2 + zl

    def send_kv(y2, zl2):
        remote(
            kv_send.at[y2 * 2 + zl2], kv_all.at[x, own_slot],
            device(x, y2, tower * 2 + zl2), 0, kv_sem.at[own_slot],
        )

    def q_for(dy, z2):
        return q_rot.at[(y + dy) % 8, (z // 6 + z2 // 6) % 2, z2 % 2]

    def place_from(dy):
        return NEAR.index((8 - dy) % 8)

    def send_q(dy, dz):
        z2 = (z + dz) % 8
        block, target = q_all.at[z, place_from(dy)], device(x, (y + dy) % 8, z2)
        remote(q_for(dy, z2), block, target, 3, qz_sem.at[z])

    def send_far_q(dy, dz):
        block = q_far.at[FAR.index((dy, dz))]
        remote(q_for(dy, (z + dz) % 8), block, device(x, (y + dy) % 8, z), 1, qy_sem.at[dy])

    def pass_far_q(dy, dz):
        block = q_far.at[FAR.index((dy, dz))]
        target = device(x, y, (z + dz) % 8)
        remote(block, q_all.at[z, place_from(dy)], target, 3, qz_sem.at[z])

    def pass_kv(pair):
        for k in (2, 1, 3):
            remote(pair, pair, device((x + k) % 4, y, z), 2, recv_sem.at[2])

    for k in (4, 3, 5, 2, 6, 1, 7):
        send_kv((y + k) % 8, zl)
        send_kv((y + k) % 8, 1 - zl)
    send_kv(y, 1 - zl)
    for dy, dz in FAR:
        send_far_q(dy, dz)
    for dy, dz in CLOSE:
        send_q(dy, dz)
    local(q_for(0, z), q_all.at[z, 0], qz_sem.at[z])
    local(kv_send.at[own_slot], kv_all.at[x, own_slot], kv_sem.at[own_slot])

    def flags(i):
        count = counts[tower * 64 + (i % 2) * 32 + (i // 16) * 8 + (i // 2) % 8]
        ones[i] = jnp.where(row < count, 1.0, 0.0).astype(jnp.bfloat16)

    arrived(kv_all.at[x, own_slot], kv_sem.at[own_slot])
    for place in range(8):
        y2 = (y + NEAR[place]) % 8
        pair = kv_all.at[x, pl.ds(2 * y2, 2)]
        for zl2 in range(2) if place else ():
            arrived(kv_all.at[x, 2 * y2 + zl2], kv_sem.at[2 * y2 + zl2])
        if place == 0:
            arrived(kv_all.at[x, y * 2 + 1 - zl], kv_sem.at[y * 2 + 1 - zl])
        pass_kv(pair)
    for dy in FAR_DY:
        arrived(q_far.at[pl.ds(0, len(FAR_DZ[dy]))], qy_sem.at[dy])
        for dz in FAR_DZ[dy]:
            pass_far_q(dy, dz)
    loop(0, 64, flags)
    arrived(kv_all.at[pl.ds(0, 3)], recv_sem.at[2])

    slot = tower * HEADS + own_slot
    keys_t[...] = jnp.transpose(kv_all[:, :, 0].reshape(64 * TOK, D))

    def attend(z2):
        queries = q_all[z2].reshape(8 * TOK, D)
        values = jnp.concatenate(
            [kv_all[:, :, 1].reshape(64 * TOK, D), ones[...].reshape(64 * TOK, D)], axis=1
        )
        scores = jnp.dot(queries, keys_t[...], preferred_element_type=jnp.float32)
        highest = jnp.max(scores, axis=1, keepdims=True)
        weights = jnp.exp2((scores - highest) * (SCALE / math.log(2.0))).astype(jnp.bfloat16)
        total = jnp.dot(weights, values, preferred_element_type=jnp.float32)
        weight_sum = total[:, D:]
        o_send[z2] = (total[:, :D] / weight_sum).astype(jnp.bfloat16).reshape(8, TOK, D)
        level = highest * SCALE + jnp.log(weight_sum)
        l_send[z2] = jnp.transpose(level)[0:1, :]

    def send_out(z2, place):
        target = device(x, (y + NEAR[place]) % 8, z2)
        remote(l_send.at[z2], l_recv.at[slot], target, 5, recv_sem.at[5])
        remote(o_send.at[z2, place], o_recv.at[slot], target, 4, recv_sem.at[4])

    def attend_group(offsets):
        for k in offsets:
            arrived(q_all.at[(z + k) % 8], qz_sem.at[(z + k) % 8])
        for k in offsets:
            attend((z + k) % 8)
        for k in offsets:
            z2 = (z + k) % 8
            for place in range(7, -1 if k else 0, -1):
                send_out(z2, place)

    attend_group((4,))
    attend_group((5, 3))
    attend_group((6, 2))
    attend_group((7, 1, 0))
    local(l_send.at[z], l_recv.at[slot], recv_sem.at[5])
    local(o_send.at[z, 0], o_recv.at[slot], recv_sem.at[4])

    arrived(l_recv, recv_sem.at[5])
    levels = l_recv[...].reshape(64, D)
    levels = jnp.transpose(jnp.concatenate([levels, levels], axis=0))
    apart = (y + 8 - lane % HEADS // 2) % 8
    place = jnp.where(apart <= 4, jnp.maximum(2 * apart - 1, 0), 16 - 2 * apart)
    mine = jnp.zeros((TOK, D), jnp.float32)
    for at in range(8):
        mine = jnp.where(place == at, levels[at * TOK:(at + 1) * TOK], mine)
    per_tower = [mine[:, t * HEADS:(t + 1) * HEADS] for t in range(3)]
    top = jnp.maximum(jnp.maximum(per_tower[0], per_tower[1]), per_tower[2])
    shares = [jnp.exp(level - top) for level in per_tower]
    share_sum = shares[0] + shares[1] + shares[2]
    shares = [share / share_sum for share in shares]
    arrived(o_recv, recv_sem.at[4])
    squares = jnp.zeros((TOK, D), jnp.float32)
    for h in range(HEADS):
        block = o_recv[3 * HEADS + h].astype(jnp.float32)
        for t in range(3):
            block += shares[t][:, h:h + 1] * o_recv[t * HEADS + h].astype(jnp.float32)
        block = jnp.where(own_valid, block, 0.0).astype(jnp.bfloat16)
        merged[h] = block
        block = block.astype(jnp.float32)
        squares += block * block

    half_heads = HEADS // 2
    remote(
        merged.at[pl.ds((1 - cfg) * half_heads, half_heads)], paired,
        {"cfg": 1 - cfg}, 6, recv_sem.at[6],
    )
    mean = jnp.sum(squares, axis=1, keepdims=True) * (1.0 / (HEADS * D))
    scale_here[...] = jnp.broadcast_to(lax.rsqrt(mean + 1e-06), (TOK, D))
    remote(scale_here, scale_there, {"cfg": 1 - cfg}, 7, recv_sem.at[7])

    def rounded(block, scale):
        return (block.astype(jnp.float32) * scale).astype(jnp.bfloat16).astype(jnp.float32)

    own_half = [
        rounded(merged[cfg * half_heads + h], scale_here[...]) for h in range(half_heads)
    ]
    arrived(paired, recv_sem.at[6])
    arrived(scale_there, recv_sem.at[7])
    for h in range(half_heads):
        there = rounded(paired[h], scale_there[...])
        conditional = jnp.where(cfg == 0, own_half[h], there)
        unconditional = jnp.where(cfg == 0, there, own_half[h])
        guided = unconditional + guide_ref[0] * (conditional - unconditional)
        out_ref[:, h * D:(h + 1) * D] = guided.astype(jnp.bfloat16)

    sent(kv_send.at[pl.ds(0, 15)], 0)
    sent(q_far, 1)
    sent(kv_all.at[pl.ds(0, 3)], 2)
    sent(o_recv.at[pl.ds(0, 63)], 3)
    sent(o_recv.at[pl.ds(0, 63)], 4)
    sent(l_recv.at[pl.ds(0, 63)], 5)
    sent(paired, 6)
    sent(scale_there, 7)


def per_device(query_self, query_cross, key_vectors, values, positions, counts, guidance):
    anywhere = pl.BlockSpec(memory_space=pltpu.HBM)
    bf16 = jnp.bfloat16
    return pl.pallas_call(
        kernel,
        out_shape=pltpu.VMEM((TOK, HEADS * D // 2), bf16),
        in_specs=[anywhere] * 6 + [pl.BlockSpec(memory_space=pltpu.SMEM)],
        out_specs=pl.BlockSpec(memory_space=pltpu.VMEM),
        scratch_shapes=[
            pltpu.VMEM((4, TOK, HEADS * D), bf16),
            pltpu.SMEM((TOK,), jnp.int32),
            pltpu.SMEM((256,), jnp.int32),
            pltpu.VMEM((64, TOK, D), bf16),
            pltpu.VMEM((HEADS, 2, TOK, D), bf16),
            pltpu.VMEM((4, HEADS, 2, TOK, D), bf16),
            pltpu.VMEM((8, 2, 2, TOK, D), bf16),
            pltpu.VMEM((len(FAR), TOK, D), bf16),
            pltpu.VMEM((8, 8, TOK, D), bf16),
            pltpu.VMEM((D, 64 * TOK), bf16),
            pltpu.VMEM((8, 8, TOK, D), bf16),
            pltpu.VMEM((64, TOK, D), bf16),
            pltpu.VMEM((8, 1, D), jnp.float32),
            pltpu.VMEM((64, 1, D), jnp.float32),
            pltpu.VMEM((HEADS, TOK, D), bf16),
            pltpu.VMEM((HEADS // 2, TOK, D), bf16),
            pltpu.VMEM((TOK, D), jnp.float32),
            pltpu.VMEM((TOK, D), jnp.float32),
            pltpu.SemaphoreType.DMA((6,)),
            pltpu.SemaphoreType.DMA((8,)),
            pltpu.SemaphoreType.DMA((8,)),
            pltpu.SemaphoreType.DMA((16,)),
            pltpu.SemaphoreType.DMA((8,)),
            pltpu.SemaphoreType.DMA((8,)),
        ],
        compiler_params=pltpu.CompilerParams(
            collective_id=0, has_side_effects=True, vmem_limit_bytes=56 * 1024 * 1024
        ),
        name="twin_attention",
    )(query_self[0], query_cross[0], key_vectors[0], values[0], positions, counts, guidance)


def solution(mesh):
    return jax.shard_map(
        per_device,
        mesh=mesh,
        in_specs=(
            P("cfg", ("tower", "seq"), None),
            P("cfg", ("tower", "seq"), None),
            P("cfg", ("tower", "seq"), None),
            P("cfg", ("tower", "seq"), None),
            P(("tower", "seq")),
            P(),
            P(),
        ),
        out_specs=P(("tower", "seq"), "cfg"),
        check_vma=False,
    )
```

```python
import math

import jax
import jax.numpy as jnp
from jax import lax
from jax.experimental import pallas as pl
from jax.experimental.pallas import tpu as pltpu
from jax.sharding import PartitionSpec as P

HEADS = 16
D = 128
TOK = 16
SCALE = 1.0 / math.sqrt(D)
NEAR = (0, 1, 7, 2, 6, 3, 5, 4)
MESH = pl.DeviceIdType.MESH


def loop(lo, hi, fn):
    def body(k, carry):
        fn(k)
        return carry

    lax.fori_loop(lo, hi, body, 0)


def device(x, y, z):
    return {"tower": z // 2, "seq": (z % 2) * 32 + x * 8 + y}


def kernel(
    qs_hbm, qc_hbm, k_hbm, v_hbm, pos_hbm, counts_hbm, guide_ref,
    out_ref,
    raw, pos, counts, ones,
    kv_send, kv_all, q_rot, q_y, q_all, keys_t, o_send, o_recv, l_send, l_recv, merged, paired, scale_here, scale_there,
    load_sem, send_sem, recv_sem, kv_sem, qy_sem, qz_sem,
):
    cfg = lax.axis_index("cfg")
    tower = lax.axis_index("tower")
    seq = lax.axis_index("seq")
    zl, x, y = seq // 32, (seq // 8) % 4, seq % 8
    z = tower * 2 + zl

    def signal(target):
        pl.semaphore_signal(barrier, inc=1, device_id=target, device_id_type=MESH)

    def remote(src, dst, target, stage, landed):
        pltpu.make_async_remote_copy(
            src_ref=src, dst_ref=dst,
            send_sem=send_sem.at[stage], recv_sem=landed,
            device_id=target, device_id_type=MESH,
        ).start()

    def local(src, dst, landed):
        pltpu.make_async_copy(src, dst, landed).start()

    def arrived(like, landed):
        pltpu.make_async_copy(like, like, landed).wait()

    def sent(like, stage):
        pltpu.make_async_copy(like, like, send_sem.at[stage]).wait()

    loads = [
        pltpu.make_async_copy(pos_hbm, pos, load_sem.at[4]),
        pltpu.make_async_copy(counts_hbm, counts, load_sem.at[5]),
        pltpu.make_async_copy(k_hbm, raw.at[2], load_sem.at[2]),
        pltpu.make_async_copy(v_hbm, raw.at[3], load_sem.at[3]),
        pltpu.make_async_copy(qs_hbm, raw.at[0], load_sem.at[0]),
        pltpu.make_async_copy(qc_hbm, raw.at[1], load_sem.at[1]),
    ]
    for copy in loads:
        copy.start()

    barrier = pltpu.get_barrier_semaphore()

    for k in (4, 3, 5, 2, 6, 1, 7):
        signal(device(x, (y + k) % 8, tower * 2 + 1 - zl))
    for k in (4, 3, 5, 2, 6, 1, 7):
        signal(device(x, (y + k) % 8, z))
        signal(device(x, y, (z + k) % 8))
    for k in (2, 1, 3):
        signal(device((x + k) % 4, y, z))
    signal({"cfg": 1 - cfg})

    for copy in loads:
        copy.wait()

    row = lax.broadcasted_iota(jnp.int32, (TOK, D), 0)
    lane = lax.broadcasted_iota(jnp.int32, (TOK, D), 1)
    time = jnp.zeros((TOK, D), jnp.int32)
    for i in range(TOK):
        time = jnp.where(row == i, pos[i], time)
    half = (lane % 64).astype(jnp.float32)
    frequency = jnp.exp(half * (-2.0 / D * math.log(10000.0)))
    angle = time.astype(jnp.float32) * frequency
    cosine = jnp.cos(angle)
    sine = jnp.where(lane < 64, -jnp.sin(angle), jnp.sin(angle))

    def rope(which, h):
        block = raw[which, :, h * D:(h + 1) * D].astype(jnp.float32)
        return block * cosine + pltpu.roll(block, 64, axis=1) * sine

    own_valid = row < counts[tower * 64 + seq]
    for h in range(HEADS):
        keys = rope(2, h)
        kv_send[h, 0] = jnp.where(own_valid, keys, keys[0:1, :]).astype(jnp.bfloat16)
        vals = raw[3, :, h * D:(h + 1) * D]
        kv_send[h, 1] = jnp.where(own_valid, vals.astype(jnp.float32), 0.0).astype(jnp.bfloat16)
    for h in range(HEADS):
        q_rot[h // 2, 0, h % 2] = rope(0, h).astype(jnp.bfloat16)
        q_rot[h // 2, 1, h % 2] = rope(1, h).astype(jnp.bfloat16)

    pl.semaphore_wait(barrier, 7 + 7 + 7 + 3 + 1)

    own_slot = y * 2 + zl

    def send_kv(y2, zl2):
        remote(
            kv_send.at[y2 * 2 + zl2], kv_all.at[x, own_slot],
            device(x, y2, tower * 2 + zl2), 0, kv_sem.at[own_slot],
        )

    def send_q(k):
        place = NEAR.index((8 - k) % 8)
        remote(q_rot.at[(y + k) % 8], q_y.at[place], device(x, (y + k) % 8, z), 1, qy_sem.at[place])

    def pass_kv(pair):
        for k in (2, 1, 3):
            remote(pair, pair, device((x + k) % 4, y, z), 2, recv_sem.at[2])

    def q_for(z2, places):
        return q_y.at[places, (z // 6 + z2 // 6) % 2, z2 % 2]

    def pass_q(first, count):
        places = pl.ds(first, count)

        for k in (4, 3, 5, 2, 6, 1, 7):
            z2 = (z + k) % 8
            remote(q_for(z2, places), q_all.at[z, places], device(x, y, z2), 3, qz_sem.at[z])

        local(q_for(z, places), q_all.at[z, places], qz_sem.at[z])

    local(q_rot.at[y], q_y.at[0], qy_sem.at[0])
    for k in (4, 3, 5, 2, 6, 1, 7):
        send_kv((y + k) % 8, zl)
        send_kv((y + k) % 8, 1 - zl)
    send_kv(y, 1 - zl)
    for k in (4, 3, 5, 2, 6, 1, 7):
        send_q(k)
    local(kv_send.at[own_slot], kv_all.at[x, own_slot], kv_sem.at[own_slot])

    def flags(i):
        count = counts[tower * 64 + (i % 2) * 32 + (i // 16) * 8 + (i // 2) % 8]
        ones[i] = jnp.where(row < count, 1.0, 0.0).astype(jnp.bfloat16)

    arrived(kv_all.at[x, own_slot], kv_sem.at[own_slot])
    arrived(q_y.at[0], qy_sem.at[0])
    for place in range(8):
        y2 = (y + NEAR[place]) % 8
        pair = kv_all.at[x, pl.ds(2 * y2, 2)]
        for zl2 in range(2) if place else ():
            arrived(kv_all.at[x, 2 * y2 + zl2], kv_sem.at[2 * y2 + zl2])
        if place == 0:
            arrived(kv_all.at[x, y * 2 + 1 - zl], kv_sem.at[y * 2 + 1 - zl])
        pass_kv(pair)
    for place in range(1, 8):
        arrived(q_y.at[place], qy_sem.at[place])
    pass_q(0, 8)
    loop(0, 64, flags)
    arrived(kv_all.at[pl.ds(0, 3)], recv_sem.at[2])

    slot = tower * HEADS + own_slot
    keys_t[...] = jnp.transpose(kv_all[:, :, 0].reshape(64 * TOK, D))

    def attend(z2):
        queries = q_all[z2].reshape(8 * TOK, D)
        values = jnp.concatenate(
            [kv_all[:, :, 1].reshape(64 * TOK, D), ones[...].reshape(64 * TOK, D)], axis=1
        )
        scores = jnp.dot(queries, keys_t[...], preferred_element_type=jnp.float32)
        highest = jnp.max(scores, axis=1, keepdims=True)
        weights = jnp.exp2((scores - highest) * (SCALE / math.log(2.0))).astype(jnp.bfloat16)
        total = jnp.dot(weights, values, preferred_element_type=jnp.float32)
        weight_sum = total[:, D:]
        o_send[z2] = (total[:, :D] / weight_sum).astype(jnp.bfloat16).reshape(8, TOK, D)
        level = highest * SCALE + jnp.log(weight_sum)
        l_send[z2] = jnp.transpose(level)[0:1, :]

    def send_out(z2, place):
        target = device(x, (y + NEAR[place]) % 8, z2)
        remote(l_send.at[z2], l_recv.at[slot], target, 5, recv_sem.at[5])
        remote(o_send.at[z2, place], o_recv.at[slot], target, 4, recv_sem.at[4])

    def attend_group(offsets):
        for k in offsets:
            arrived(q_all.at[(z + k) % 8], qz_sem.at[(z + k) % 8])
        for k in offsets:
            attend((z + k) % 8)
        for k in offsets:
            z2 = (z + k) % 8
            for place in range(7, -1 if k else 0, -1):
                send_out(z2, place)

    attend_group((4,))
    attend_group((5, 3))
    attend_group((6, 2))
    attend_group((7, 1, 0))
    local(l_send.at[z], l_recv.at[slot], recv_sem.at[5])
    local(o_send.at[z, 0], o_recv.at[slot], recv_sem.at[4])

    arrived(l_recv, recv_sem.at[5])
    levels = l_recv[...].reshape(64, D)
    levels = jnp.transpose(jnp.concatenate([levels, levels], axis=0))
    apart = (y + 8 - lane % HEADS // 2) % 8
    place = jnp.where(apart <= 4, jnp.maximum(2 * apart - 1, 0), 16 - 2 * apart)
    mine = jnp.zeros((TOK, D), jnp.float32)
    for at in range(8):
        mine = jnp.where(place == at, levels[at * TOK:(at + 1) * TOK], mine)
    per_tower = [mine[:, t * HEADS:(t + 1) * HEADS] for t in range(3)]
    top = jnp.maximum(jnp.maximum(per_tower[0], per_tower[1]), per_tower[2])
    shares = [jnp.exp(level - top) for level in per_tower]
    share_sum = shares[0] + shares[1] + shares[2]
    shares = [share / share_sum for share in shares]
    arrived(o_recv, recv_sem.at[4])
    squares = jnp.zeros((TOK, D), jnp.float32)
    for h in range(HEADS):
        block = o_recv[3 * HEADS + h].astype(jnp.float32)
        for t in range(3):
            block += shares[t][:, h:h + 1] * o_recv[t * HEADS + h].astype(jnp.float32)
        block = jnp.where(own_valid, block, 0.0).astype(jnp.bfloat16)
        merged[h] = block
        block = block.astype(jnp.float32)
        squares += block * block

    half_heads = HEADS // 2
    remote(
        merged.at[pl.ds((1 - cfg) * half_heads, half_heads)], paired,
        {"cfg": 1 - cfg}, 6, recv_sem.at[6],
    )
    mean = jnp.sum(squares, axis=1, keepdims=True) * (1.0 / (HEADS * D))
    scale_here[...] = jnp.broadcast_to(lax.rsqrt(mean + 1e-06), (TOK, D))
    remote(scale_here, scale_there, {"cfg": 1 - cfg}, 7, recv_sem.at[7])

    def rounded(block, scale):
        return (block.astype(jnp.float32) * scale).astype(jnp.bfloat16).astype(jnp.float32)

    own_half = [
        rounded(merged[cfg * half_heads + h], scale_here[...]) for h in range(half_heads)
    ]
    arrived(paired, recv_sem.at[6])
    arrived(scale_there, recv_sem.at[7])
    for h in range(half_heads):
        there = rounded(paired[h], scale_there[...])
        conditional = jnp.where(cfg == 0, own_half[h], there)
        unconditional = jnp.where(cfg == 0, there, own_half[h])
        guided = unconditional + guide_ref[0] * (conditional - unconditional)
        out_ref[:, h * D:(h + 1) * D] = guided.astype(jnp.bfloat16)

    sent(kv_send.at[pl.ds(0, 15)], 0)
    sent(q_y.at[pl.ds(0, 7)], 1)
    sent(kv_all.at[pl.ds(0, 3)], 2)
    sent(q_all.at[pl.ds(0, 7)], 3)
    sent(o_recv.at[pl.ds(0, 63)], 4)
    sent(l_recv.at[pl.ds(0, 63)], 5)
    sent(paired, 6)
    sent(scale_there, 7)


def per_device(query_self, query_cross, key_vectors, values, positions, counts, guidance):
    anywhere = pl.BlockSpec(memory_space=pltpu.HBM)
    bf16 = jnp.bfloat16
    return pl.pallas_call(
        kernel,
        out_shape=pltpu.VMEM((TOK, HEADS * D // 2), bf16),
        in_specs=[anywhere] * 6 + [pl.BlockSpec(memory_space=pltpu.SMEM)],
        out_specs=pl.BlockSpec(memory_space=pltpu.VMEM),
        scratch_shapes=[
            pltpu.VMEM((4, TOK, HEADS * D), bf16),
            pltpu.SMEM((TOK,), jnp.int32),
            pltpu.SMEM((256,), jnp.int32),
            pltpu.VMEM((64, TOK, D), bf16),
            pltpu.VMEM((HEADS, 2, TOK, D), bf16),
            pltpu.VMEM((4, HEADS, 2, TOK, D), bf16),
            pltpu.VMEM((8, 2, 2, TOK, D), bf16),
            pltpu.VMEM((8, 2, 2, TOK, D), bf16),
            pltpu.VMEM((8, 8, TOK, D), bf16),
            pltpu.VMEM((D, 64 * TOK), bf16),
            pltpu.VMEM((8, 8, TOK, D), bf16),
            pltpu.VMEM((64, TOK, D), bf16),
            pltpu.VMEM((8, 1, D), jnp.float32),
            pltpu.VMEM((64, 1, D), jnp.float32),
            pltpu.VMEM((HEADS, TOK, D), bf16),
            pltpu.VMEM((HEADS // 2, TOK, D), bf16),
            pltpu.VMEM((TOK, D), jnp.float32),
            pltpu.VMEM((TOK, D), jnp.float32),
            pltpu.SemaphoreType.DMA((6,)),
            pltpu.SemaphoreType.DMA((8,)),
            pltpu.SemaphoreType.DMA((8,)),
            pltpu.SemaphoreType.DMA((16,)),
            pltpu.SemaphoreType.DMA((8,)),
            pltpu.SemaphoreType.DMA((8,)),
        ],
        compiler_params=pltpu.CompilerParams(
            collective_id=0, has_side_effects=True, vmem_limit_bytes=56 * 1024 * 1024
        ),
        name="twin_attention",
    )(query_self[0], query_cross[0], key_vectors[0], values[0], positions, counts, guidance)


def solution(mesh):
    return jax.shard_map(
        per_device,
        mesh=mesh,
        in_specs=(
            P("cfg", ("tower", "seq"), None),
            P("cfg", ("tower", "seq"), None),
            P("cfg", ("tower", "seq"), None),
            P("cfg", ("tower", "seq"), None),
            P(("tower", "seq")),
            P(),
            P(),
        ),
        out_specs=P(("tower", "seq"), "cfg"),
        check_vma=False,
    )
```

```python
import math

import jax
import jax.numpy as jnp
from jax import lax
from jax.experimental import pallas as pl
from jax.experimental.pallas import tpu as pltpu
from jax.sharding import PartitionSpec as P

HEADS = 16
D = 128
TOK = 16
SCALE = 1.0 / math.sqrt(D)
NEAR = (0, 1, 7, 2, 6, 3, 5, 4)
MESH = pl.DeviceIdType.MESH


def loop(lo, hi, fn):
    def body(k, carry):
        fn(k)
        return carry

    lax.fori_loop(lo, hi, body, 0)


def device(x, y, z):
    return {"tower": z // 2, "seq": (z % 2) * 32 + x * 8 + y}


def kernel(
    qs_hbm, qc_hbm, k_hbm, v_hbm, pos_hbm, counts_hbm, guide_ref,
    out_ref,
    raw, pos, counts, ones,
    kv_send, kv_all, q_rot, q_y, q_all, keys_t, o_send, o_recv, l_send, l_recv, merged, paired, scale_here, scale_there,
    load_sem, send_sem, recv_sem, kv_sem, qy_sem, qz_sem, x_sem,
):
    cfg = lax.axis_index("cfg")
    tower = lax.axis_index("tower")
    seq = lax.axis_index("seq")
    zl, x, y = seq // 32, (seq // 8) % 4, seq % 8
    z = tower * 2 + zl

    def signal(target):
        pl.semaphore_signal(barrier, inc=1, device_id=target, device_id_type=MESH)

    def remote(src, dst, target, stage, landed):
        pltpu.make_async_remote_copy(
            src_ref=src, dst_ref=dst,
            send_sem=send_sem.at[stage], recv_sem=landed,
            device_id=target, device_id_type=MESH,
        ).start()

    def local(src, dst, landed):
        pltpu.make_async_copy(src, dst, landed).start()

    def arrived(like, landed):
        pltpu.make_async_copy(like, like, landed).wait()

    def sent(like, stage):
        pltpu.make_async_copy(like, like, send_sem.at[stage]).wait()

    loads = [
        pltpu.make_async_copy(pos_hbm, pos, load_sem.at[4]),
        pltpu.make_async_copy(counts_hbm, counts, load_sem.at[5]),
        pltpu.make_async_copy(k_hbm, raw.at[2], load_sem.at[2]),
        pltpu.make_async_copy(v_hbm, raw.at[3], load_sem.at[3]),
        pltpu.make_async_copy(qs_hbm, raw.at[0], load_sem.at[0]),
        pltpu.make_async_copy(qc_hbm, raw.at[1], load_sem.at[1]),
    ]
    for copy in loads:
        copy.start()

    barrier = pltpu.get_barrier_semaphore()

    for k in (4, 3, 5, 2, 6, 1, 7):
        signal(device(x, (y + k) % 8, tower * 2 + 1 - zl))
    for k in (4, 3, 5, 2, 6, 1, 7):
        signal(device(x, (y + k) % 8, z))
        signal(device(x, y, (z + k) % 8))
    for k in (2, 1, 3):
        signal(device((x + k) % 4, y, z))
    signal({"cfg": 1 - cfg})

    for copy in loads:
        copy.wait()

    row = lax.broadcasted_iota(jnp.int32, (TOK, D), 0)
    lane = lax.broadcasted_iota(jnp.int32, (TOK, D), 1)
    time = jnp.zeros((TOK, D), jnp.int32)
    for i in range(TOK):
        time = jnp.where(row == i, pos[i], time)
    half = (lane % 64).astype(jnp.float32)
    frequency = jnp.exp(half * (-2.0 / D * math.log(10000.0)))
    angle = time.astype(jnp.float32) * frequency
    cosine = jnp.cos(angle)
    sine = jnp.where(lane < 64, -jnp.sin(angle), jnp.sin(angle))

    def rope(which, h):
        block = raw[which, :, h * D:(h + 1) * D].astype(jnp.float32)
        return block * cosine + pltpu.roll(block, 64, axis=1) * sine

    own_valid = row < counts[tower * 64 + seq]
    for h in range(HEADS):
        keys = rope(2, h)
        kv_send[h, 0] = jnp.where(own_valid, keys, keys[0:1, :]).astype(jnp.bfloat16)
        vals = raw[3, :, h * D:(h + 1) * D]
        kv_send[h, 1] = jnp.where(own_valid, vals.astype(jnp.float32), 0.0).astype(jnp.bfloat16)
    for h in range(HEADS):
        q_rot[h // 2, 0, h % 2] = rope(0, h).astype(jnp.bfloat16)
        q_rot[h // 2, 1, h % 2] = rope(1, h).astype(jnp.bfloat16)

    pl.semaphore_wait(barrier, 7 + 7 + 7 + 3 + 1)

    own_slot = y * 2 + zl

    def send_kv(y2, zl2):
        remote(
            kv_send.at[y2 * 2 + zl2], kv_all.at[x, own_slot],
            device(x, y2, tower * 2 + zl2), 0, kv_sem.at[own_slot],
        )

    def send_q(k):
        place = NEAR.index((8 - k) % 8)
        remote(q_rot.at[(y + k) % 8], q_y.at[place], device(x, (y + k) % 8, z), 1, qy_sem.at[place])

    def pass_kv(pair):
        for k in (2, 1, 3):
            remote(pair, pair, device((x + k) % 4, y, z), 2, x_sem.at[x])

    def q_for(z2, places):
        return q_y.at[places, (z // 6 + z2 // 6) % 2, z2 % 2]

    def pass_q(first, count):
        places = pl.ds(first, count)

        for k in (4, 3, 5, 2, 6, 1, 7):
            z2 = (z + k) % 8
            remote(q_for(z2, places), q_all.at[z, places], device(x, y, z2), 3, qz_sem.at[z])

        local(q_for(z, places), q_all.at[z, places], qz_sem.at[z])

    local(q_rot.at[y], q_y.at[0], qy_sem.at[0])
    for k in (4, 3, 5, 2, 6, 1, 7):
        send_kv((y + k) % 8, zl)
        send_kv((y + k) % 8, 1 - zl)
    send_kv(y, 1 - zl)
    for k in (4, 3, 5, 2, 6, 1, 7):
        send_q(k)
    local(kv_send.at[own_slot], kv_all.at[x, own_slot], kv_sem.at[own_slot])

    def flags(i):
        count = counts[tower * 64 + (i % 2) * 32 + (i // 16) * 8 + (i // 2) % 8]
        ones[i] = jnp.where(row < count, 1.0, 0.0).astype(jnp.bfloat16)

    arrived(kv_all.at[x, own_slot], kv_sem.at[own_slot])
    arrived(q_y.at[0], qy_sem.at[0])
    for place in range(8):
        y2 = (y + NEAR[place]) % 8
        pair = kv_all.at[x, pl.ds(2 * y2, 2)]
        for zl2 in range(2) if place else ():
            arrived(kv_all.at[x, 2 * y2 + zl2], kv_sem.at[2 * y2 + zl2])
        if place == 0:
            arrived(kv_all.at[x, y * 2 + 1 - zl], kv_sem.at[y * 2 + 1 - zl])
        pass_kv(pair)
    for place in range(1, 8):
        arrived(q_y.at[place], qy_sem.at[place])
    pass_q(0, 8)
    loop(0, 64, flags)

    def turn(x2):
        keys_t[x2] = jnp.transpose(kv_all[x2, :, 0].reshape(16 * TOK, D))

    turn(x)
    for k in (1, 3, 2):
        x2 = (x + k) % 4
        arrived(kv_all.at[x2], x_sem.at[x2])
        turn(x2)

    slot = tower * HEADS + own_slot

    def attend(z2):
        queries = q_all[z2].reshape(8 * TOK, D)
        keys = jnp.concatenate([keys_t[i] for i in range(4)], axis=1)
        values = jnp.concatenate(
            [kv_all[:, :, 1].reshape(64 * TOK, D), ones[...].reshape(64 * TOK, D)], axis=1
        )
        scores = jnp.dot(queries, keys, preferred_element_type=jnp.float32)
        highest = jnp.max(scores, axis=1, keepdims=True)
        weights = jnp.exp2((scores - highest) * (SCALE / math.log(2.0))).astype(jnp.bfloat16)
        total = jnp.dot(weights, values, preferred_element_type=jnp.float32)
        weight_sum = total[:, D:]
        o_send[z2] = (total[:, :D] / weight_sum).astype(jnp.bfloat16).reshape(8, TOK, D)
        level = highest * SCALE + jnp.log(weight_sum)
        l_send[z2] = jnp.transpose(level)[0:1, :]

    def send_out(z2, place):
        target = device(x, (y + NEAR[place]) % 8, z2)
        remote(l_send.at[z2], l_recv.at[slot], target, 5, recv_sem.at[5])
        remote(o_send.at[z2, place], o_recv.at[slot], target, 4, recv_sem.at[4])

    def attend_group(offsets):
        for k in offsets:
            arrived(q_all.at[(z + k) % 8], qz_sem.at[(z + k) % 8])
        for k in offsets:
            attend((z + k) % 8)
        for k in offsets:
            z2 = (z + k) % 8
            for place in range(7, -1 if k else 0, -1):
                send_out(z2, place)

    attend_group((4,))
    attend_group((5, 3))
    attend_group((6, 2))
    attend_group((7, 1, 0))
    local(l_send.at[z], l_recv.at[slot], recv_sem.at[5])
    local(o_send.at[z, 0], o_recv.at[slot], recv_sem.at[4])

    arrived(l_recv, recv_sem.at[5])
    levels = l_recv[...].reshape(64, D)
    levels = jnp.transpose(jnp.concatenate([levels, levels], axis=0))
    apart = (y + 8 - lane % HEADS // 2) % 8
    place = jnp.where(apart <= 4, jnp.maximum(2 * apart - 1, 0), 16 - 2 * apart)
    mine = jnp.zeros((TOK, D), jnp.float32)
    for at in range(8):
        mine = jnp.where(place == at, levels[at * TOK:(at + 1) * TOK], mine)
    per_tower = [mine[:, t * HEADS:(t + 1) * HEADS] for t in range(3)]
    top = jnp.maximum(jnp.maximum(per_tower[0], per_tower[1]), per_tower[2])
    shares = [jnp.exp(level - top) for level in per_tower]
    share_sum = shares[0] + shares[1] + shares[2]
    shares = [share / share_sum for share in shares]
    arrived(o_recv, recv_sem.at[4])
    squares = jnp.zeros((TOK, D), jnp.float32)
    for h in range(HEADS):
        block = o_recv[3 * HEADS + h].astype(jnp.float32)
        for t in range(3):
            block += shares[t][:, h:h + 1] * o_recv[t * HEADS + h].astype(jnp.float32)
        block = jnp.where(own_valid, block, 0.0).astype(jnp.bfloat16)
        merged[h] = block
        block = block.astype(jnp.float32)
        squares += block * block

    half_heads = HEADS // 2
    remote(
        merged.at[pl.ds((1 - cfg) * half_heads, half_heads)], paired,
        {"cfg": 1 - cfg}, 6, recv_sem.at[6],
    )
    mean = jnp.sum(squares, axis=1, keepdims=True) * (1.0 / (HEADS * D))
    scale_here[...] = jnp.broadcast_to(lax.rsqrt(mean + 1e-06), (TOK, D))
    remote(scale_here, scale_there, {"cfg": 1 - cfg}, 7, recv_sem.at[7])

    def rounded(block, scale):
        return (block.astype(jnp.float32) * scale).astype(jnp.bfloat16).astype(jnp.float32)

    own_half = [
        rounded(merged[cfg * half_heads + h], scale_here[...]) for h in range(half_heads)
    ]
    arrived(paired, recv_sem.at[6])
    arrived(scale_there, recv_sem.at[7])
    for h in range(half_heads):
        there = rounded(paired[h], scale_there[...])
        conditional = jnp.where(cfg == 0, own_half[h], there)
        unconditional = jnp.where(cfg == 0, there, own_half[h])
        guided = unconditional + guide_ref[0] * (conditional - unconditional)
        out_ref[:, h * D:(h + 1) * D] = guided.astype(jnp.bfloat16)

    sent(kv_send.at[pl.ds(0, 15)], 0)
    sent(q_y.at[pl.ds(0, 7)], 1)
    sent(kv_all.at[pl.ds(0, 3)], 2)
    sent(q_all.at[pl.ds(0, 7)], 3)
    sent(o_recv.at[pl.ds(0, 63)], 4)
    sent(l_recv.at[pl.ds(0, 63)], 5)
    sent(paired, 6)
    sent(scale_there, 7)


def per_device(query_self, query_cross, key_vectors, values, positions, counts, guidance):
    anywhere = pl.BlockSpec(memory_space=pltpu.HBM)
    bf16 = jnp.bfloat16
    return pl.pallas_call(
        kernel,
        out_shape=pltpu.VMEM((TOK, HEADS * D // 2), bf16),
        in_specs=[anywhere] * 6 + [pl.BlockSpec(memory_space=pltpu.SMEM)],
        out_specs=pl.BlockSpec(memory_space=pltpu.VMEM),
        scratch_shapes=[
            pltpu.VMEM((4, TOK, HEADS * D), bf16),
            pltpu.SMEM((TOK,), jnp.int32),
            pltpu.SMEM((256,), jnp.int32),
            pltpu.VMEM((64, TOK, D), bf16),
            pltpu.VMEM((HEADS, 2, TOK, D), bf16),
            pltpu.VMEM((4, HEADS, 2, TOK, D), bf16),
            pltpu.VMEM((8, 2, 2, TOK, D), bf16),
            pltpu.VMEM((8, 2, 2, TOK, D), bf16),
            pltpu.VMEM((8, 8, TOK, D), bf16),
            pltpu.VMEM((4, D, 16 * TOK), bf16),
            pltpu.VMEM((8, 8, TOK, D), bf16),
            pltpu.VMEM((64, TOK, D), bf16),
            pltpu.VMEM((8, 1, D), jnp.float32),
            pltpu.VMEM((64, 1, D), jnp.float32),
            pltpu.VMEM((HEADS, TOK, D), bf16),
            pltpu.VMEM((HEADS // 2, TOK, D), bf16),
            pltpu.VMEM((TOK, D), jnp.float32),
            pltpu.VMEM((TOK, D), jnp.float32),
            pltpu.SemaphoreType.DMA((6,)),
            pltpu.SemaphoreType.DMA((8,)),
            pltpu.SemaphoreType.DMA((8,)),
            pltpu.SemaphoreType.DMA((16,)),
            pltpu.SemaphoreType.DMA((8,)),
            pltpu.SemaphoreType.DMA((8,)),
            pltpu.SemaphoreType.DMA((4,)),
        ],
        compiler_params=pltpu.CompilerParams(
            collective_id=0, has_side_effects=True, vmem_limit_bytes=56 * 1024 * 1024
        ),
        name="twin_attention",
    )(query_self[0], query_cross[0], key_vectors[0], values[0], positions, counts, guidance)


def solution(mesh):
    return jax.shard_map(
        per_device,
        mesh=mesh,
        in_specs=(
            P("cfg", ("tower", "seq"), None),
            P("cfg", ("tower", "seq"), None),
            P("cfg", ("tower", "seq"), None),
            P("cfg", ("tower", "seq"), None),
            P(("tower", "seq")),
            P(),
            P(),
        ),
        out_specs=P(("tower", "seq"), "cfg"),
        check_vma=False,
    )
```
